32 devices in a mesh: dp: 8 (over z, x), seq: 4 (over y, core).
Axes of the slice: x: 2, y: 2, z: 4, core: 2. Of those that a mesh axis runs over, the one named last changes fastest.
Arguments:
- hidden_in: bfloat16 [4096, 1024], P(('dp', 'seq')), may hold values from -6 to 6
- cotangent: bfloat16 [4096, 1024], P(('dp', 'seq')), may hold values from -6 to 6
- segments: int32 [8, 512], P('dp'), may hold values from 0 to 2, never falling along the last dimension, each value on 1 to 256 neighbouring positions
- shared_params: float32 [9216], P(('dp', 'seq')), as said below
- split_params: float32 [4, 3146752], P('seq', 'dp'), as said below
- shared_m1: float32 [9216], P(('dp', 'seq')), may hold values from -56 to 56
- split_m1: float32 [4, 3146752], P('seq', 'dp'), may hold values from -56 to 56
- shared_m2: float32 [9216], P(('dp', 'seq')), may hold values from 204.8 to 819.2
- split_m2: float32 [4, 3146752], P('seq', 'dp'), may hold values from 204.8 to 819.2
Outputs:
- output: bfloat16 [4096, 1024], P(('dp', 'seq'))
- input_grad: float32 [4096, 1024], P(('dp', 'seq'))
- shared_grads: float32 [9216], P(('dp', 'seq'))
- split_grads: float32 [4, 3146752], P('seq', 'dp')
- shared_new: float32 [9216], P(('dp', 'seq'))
- split_new: float32 [4, 3146752], P('seq', 'dp')
- shared_m1_new: float32 [9216], P(('dp', 'seq'))
- split_m1_new: float32 [4, 3146752], P('seq', 'dp')
- shared_m2_new: float32 [9216], P(('dp', 'seq'))
- split_m2_new: float32 [4, 3146752], P('seq', 'dp')
The draws below stay inside these ranges and needn't reach their ends.
Inputs may be any that keep to these rules, and one draw needn't show every extreme that they name: `shared_params`: the 9216 entries are the shared parameters packed as the first step reads them. `split_params`: row s holds the share s of the qkv, dense, fc and proj parameters as the second step reads them.
All inputs are finite; a program needn't handle non-finite values.
Results may differ from the reference program's by a relative error of at most 0.007.
The reference program's roundings to bfloat16 on the way count: a program that leaves them out, or rounds other values in their place, can miss the bound.
Values may be sent and summed in bfloat16 or wider, within the bound.
A program may use at most 192 MiB of HBM per device.

```python
import math
import jax
import jax.numpy as jnp
import numpy as np
from jax import lax

MODEL_WIDTH = 1024
HEADS = 16
HEAD_DIM = 64
FF = 4096
ROT = 16
STEP = 3
GROUP = 512
TOKENS = 4096
SHARED = 9216
SPLIT = 3146752
N_DP = 8
N_SEQ = 4


def normal_piece(base_key, index, extent):
    return jnp.clip(jax.random.normal(jax.random.fold_in(base_key, index), extent, jnp.float32), -4.0, 4.0)


def draw_shared_params(key, part):
    b_qkv = normal_piece(key, 1, (3 * MODEL_WIDTH,)) * 0.5
    b_dense = normal_piece(key, 3, (MODEL_WIDTH,)) * 0.5
    b_proj = normal_piece(key, 7, (MODEL_WIDTH,)) * 0.5
    gain_one = 1.0 + jax.random.uniform(jax.random.fold_in(key, 8), (MODEL_WIDTH,), jnp.float32, -0.4, 0.4)
    shift_one = normal_piece(key, 9, (MODEL_WIDTH,)) * 0.3
    gain_two = 1.0 + jax.random.uniform(jax.random.fold_in(key, 10), (MODEL_WIDTH,), jnp.float32, -0.4, 0.4)
    shift_two = normal_piece(key, 11, (MODEL_WIDTH,)) * 0.3
    return jnp.concatenate([b_qkv, b_dense, b_proj, gain_one, shift_one, gain_two, shift_two])


def draw_split_params(key, part):
    qkv_part = 3 * MODEL_WIDTH // N_SEQ
    dense_output_slice = MODEL_WIDTH // N_SEQ
    hidden_units_slice = FF // N_SEQ
    w_qkv = normal_piece(key, 0, (MODEL_WIDTH, 3 * MODEL_WIDTH)) * MODEL_WIDTH ** (-0.5)
    dense_weight = normal_piece(key, 2, (MODEL_WIDTH, MODEL_WIDTH)) * (8.0 * MODEL_WIDTH ** (-0.5))
    expand_weight = normal_piece(key, 4, (MODEL_WIDTH, FF)) * (3.0 * MODEL_WIDTH ** (-0.5))
    b_fc = normal_piece(key, 5, (FF,)) * 0.5
    contract_weight = normal_piece(key, 6, (FF, MODEL_WIDTH)) * (1.5 * FF ** (-0.5))
    return jnp.concatenate([w_qkv.reshape(MODEL_WIDTH, N_SEQ, qkv_part).transpose(1, 0, 2).reshape(N_SEQ, MODEL_WIDTH * qkv_part), dense_weight.reshape(N_SEQ, dense_output_slice * MODEL_WIDTH), expand_weight.reshape(MODEL_WIDTH, N_SEQ, hidden_units_slice).transpose(1, 0, 2).reshape(N_SEQ, MODEL_WIDTH * hidden_units_slice), b_fc.reshape(N_SEQ, hidden_units_slice), contract_weight.reshape(N_SEQ, hidden_units_slice * MODEL_WIDTH)], 1)


def levels(key, shape, split, least, top_value):
    level = 1.0
    for dim, shards_of in split:
        draws = jax.random.uniform(jax.random.fold_in(jax.random.fold_in(key, 6), dim), (shards_of,), jnp.float32, least / len(split), top_value / len(split))
        level = level * jnp.repeat(jnp.exp(draws), shape[dim] // shards_of).reshape((-1,) + (1,) * (len(shape) - 1 - dim))
    return level


def profile(number_of, total, reach, skew):
    portions = [(1 << 20) // math.isqrt(rank ** skew) + 1 for rank in range(2, number_of + 1)]
    surplus, given = total - reach - (number_of - 1), [1] * (number_of - 1)
    while surplus > 0:
        movable = [i for i in range(number_of - 1) if given[i] < reach]
        mass, left = sum([portions[i] for i in movable]), surplus
        for i in movable:
            addition = min(reach - given[i], max(1, left * portions[i] // mass), surplus)
            given[i] = given[i] + addition
            surplus = surplus - addition
    return np.array([reach] + given)


def ragged_sizes(key, count, total, bound, skew):
    if count == 2:
        one = jax.random.randint(key, (), max(1, total - bound), min(bound, total - 1) + 1)
        return jnp.stack([one, total - one])
    sizes = jnp.asarray(profile(count, total, bound, skew), jnp.int32)
    pairs = (count - 1) // 2
    source_of, taker = sizes[1:1 + 2 * pairs:2], sizes[2:2 + 2 * pairs:2]
    room = jnp.minimum(source_of - 1, bound - taker)
    moved = jax.random.randint(jax.random.fold_in(key, 1), (pairs,), 0, 1 << 20) % (room + 1)
    sizes = sizes.at[1:1 + 2 * pairs:2].set(source_of - moved).at[2:2 + 2 * pairs:2].set(taker + moved)
    return sizes[jax.random.permutation(jax.random.fold_in(key, 2), count)]


def bell_draw(stream_key, dims, spread, limit, shards=(), kind=jnp.bfloat16):
    gain = levels(stream_key, dims, shards, -0.22, 0.18) if shards else 1.0
    array = jax.random.normal(stream_key, dims, jnp.float32) * spread * gain
    return jnp.minimum(jnp.maximum(array, -limit), limit).astype(kind)


def setup_inputs(seed: int = 0) -> dict:
    key_list = jax.random.split(jax.random.key(seed), 10)
    hidden_in = bell_draw(key_list[0], (TOKENS, MODEL_WIDTH), 1.0, 6.0, ((0, 32),))
    cotangent = bell_draw(key_list[1], (TOKENS, MODEL_WIDTH), 1.0, 6.0, ((0, 32),))
    segments = jax.vmap(lambda own: jnp.searchsorted(jnp.cumsum(ragged_sizes(own, 3, GROUP, GROUP // 2, 2)), jnp.arange(GROUP), side="right"))(jax.random.split(key_list[2], N_DP)).reshape((N_DP, GROUP)).astype(jnp.int32)
    shared_params = draw_shared_params(jax.random.fold_in(key_list[9], 71), 0)
    split_params = draw_split_params(jax.random.fold_in(key_list[9], 71), 0)
    shared_m1 = bell_draw(key_list[5], (SHARED,), (0.15 * TOKENS ** 0.5), 56.0, ((0, 32),), jnp.float32)
    split_m1 = bell_draw(key_list[6], (N_SEQ, SPLIT), (0.15 * TOKENS ** 0.5), 56.0, ((0, 4), (1, 8)), jnp.float32)
    shared_m2 = jnp.clip(jnp.exp(math.log(819.2) - 1.3862944 * jax.random.uniform(key_list[7], (SHARED,), jnp.float32) ** levels(key_list[7], (SHARED,), ((0, 32),), -0.2, 0.2)), 204.8, 819.2)
    split_m2 = jnp.clip(jnp.exp(math.log(819.2) - 1.3862944 * jax.random.uniform(key_list[8], (N_SEQ, SPLIT), jnp.float32) ** levels(key_list[8], (N_SEQ, SPLIT), ((0, 4), (1, 8)), -0.2, 0.2)), 204.8, 819.2)
    return {"hidden_in": hidden_in, "cotangent": cotangent, "segments": segments, "shared_params": shared_params, "split_params": split_params, "shared_m1": shared_m1, "split_m1": split_m1, "shared_m2": shared_m2, "split_m2": split_m2}


norm_eps = 1e-05
beta_first = 0.9
beta_second = 0.95
adam_eps = 1e-08
learn_rate = 0.1
weight_decay = 0.01
rotary_base = 10000.0
masked_score = -1e+30

def unpack_shared(flat_vec):
    extents = [(3 * MODEL_WIDTH,), (MODEL_WIDTH,), (MODEL_WIDTH,), (MODEL_WIDTH,), (MODEL_WIDTH,), (MODEL_WIDTH,), (MODEL_WIDTH,)]
    pieces = []
    offset = 0
    for extent in extents:
        number = math.prod(extent)
        pieces.append(flat_vec[offset:offset + number].reshape(extent))
        offset = offset + number
    return pieces

def unpack_split(matrix, seq_count):
    rows = matrix.shape[0]
    qkv_part = 3 * MODEL_WIDTH // seq_count
    dense_output_slice = MODEL_WIDTH // seq_count
    hidden_units_slice = FF // seq_count
    zero_end = MODEL_WIDTH * qkv_part
    first_end = zero_end + dense_output_slice * MODEL_WIDTH
    second_end = first_end + MODEL_WIDTH * hidden_units_slice
    third_end = second_end + hidden_units_slice
    w_qkv = matrix[:, :zero_end].reshape(rows, MODEL_WIDTH, qkv_part).transpose(1, 0, 2).reshape(MODEL_WIDTH, rows * qkv_part)
    dense_weight = matrix[:, zero_end:first_end].reshape(rows * dense_output_slice, MODEL_WIDTH)
    expand_weight = matrix[:, first_end:second_end].reshape(rows, MODEL_WIDTH, hidden_units_slice).transpose(1, 0, 2).reshape(MODEL_WIDTH, rows * hidden_units_slice)
    b_fc = matrix[:, second_end:third_end].reshape(rows * hidden_units_slice)
    contract_weight = matrix[:, third_end:].reshape(rows * hidden_units_slice, MODEL_WIDTH)
    return (w_qkv, dense_weight, expand_weight, b_fc, contract_weight)

def pack_split(w_qkv, dense_weight, expand_weight, b_fc, contract_weight, seq_count):
    qkv_part = 3 * MODEL_WIDTH // seq_count
    dense_output_slice = MODEL_WIDTH // seq_count
    hidden_units_slice = FF // seq_count
    rows = dense_weight.shape[0] // dense_output_slice
    return jnp.concatenate([w_qkv.reshape(MODEL_WIDTH, rows, qkv_part).transpose(1, 0, 2).reshape(rows, MODEL_WIDTH * qkv_part), dense_weight.reshape(rows, dense_output_slice * MODEL_WIDTH), expand_weight.reshape(MODEL_WIDTH, rows, hidden_units_slice).transpose(1, 0, 2).reshape(rows, MODEL_WIDTH * hidden_units_slice), b_fc.reshape(rows, hidden_units_slice), contract_weight.reshape(rows, hidden_units_slice * MODEL_WIDTH)], 1)

def adamw(param_vals, first_m, second_m, grad_vals):
    first_new = beta_first * first_m + (1.0 - beta_first) * grad_vals
    second_new = beta_second * second_m + (1.0 - beta_second) * grad_vals * grad_vals
    first_hat = first_new / (1.0 - beta_first ** STEP)
    second_hat = second_new / (1.0 - beta_second ** STEP)
    param_new = param_vals - learn_rate * (first_hat / (jnp.sqrt(second_hat) + adam_eps) + weight_decay * param_vals)
    return (param_new, first_new, second_new)

def layer_norm(resid, gain_vec, shift_vec):
    average = lax.optimization_barrier(jnp.mean(resid, -1, keepdims=True))
    centered = resid - average
    variance = lax.optimization_barrier(jnp.mean(centered * centered, -1, keepdims=True))
    recip_root = lax.rsqrt(variance + norm_eps)
    normed = centered * recip_root
    return (normed * gain_vec + shift_vec, normed, recip_root)

def norm_back(grad_norm, gain_vec, normed, recip_root):
    scaled = grad_norm * gain_vec
    return recip_root * (scaled - lax.optimization_barrier(jnp.mean(scaled, -1, keepdims=True)) - normed * lax.optimization_barrier(jnp.mean(scaled * normed, -1, keepdims=True)))

def gelu_slope(inputs):
    normal_cdf = 0.5 * (1.0 + jax.scipy.special.erf(inputs * 0.7071067811865476))
    return normal_cdf + inputs * jnp.exp(-0.5 * inputs * inputs) * 0.3989422804014327

def rotary_tables(segment_row):
    indices = jnp.arange(segment_row.shape[0], dtype=jnp.int32)
    change = jnp.concatenate([jnp.ones((1,), dtype=jnp.bool_), segment_row[1:] != segment_row[:-1]])
    starts = lax.cummax(jnp.where(change, indices, jnp.zeros_like(indices)), axis=0)
    positions = (indices - starts).astype(jnp.float32)
    frequency = rotary_base ** (-jnp.arange(0, ROT, 2, dtype=jnp.float32) / ROT)
    angles = positions[:, None] * frequency[None, :]
    return (jnp.cos(angles)[:, None, :], jnp.sin(angles)[:, None, :])

def rotate(field, cosines, sines, direction):
    half_rot = ROT // 2
    first_half = field[..., :half_rot]
    second = field[..., half_rot:ROT]
    return jnp.concatenate([first_half * cosines - direction * second * sines, second * cosines + direction * first_half * sines, field[..., ROT:]], -1)

def score_block(query_block, keys_rot, seg_block, row_ids, segment_row, col_ids):
    scale = HEAD_DIM ** (-0.5)
    scores = jnp.einsum('ihd,jhd->hij', query_block.astype(jnp.float32), keys_rot.astype(jnp.float32)) * scale
    allowed = (seg_block[:, None] == segment_row[None, :]) & (row_ids[:, None] >= col_ids[None, :])
    return jnp.where(allowed[None], scores, masked_score)

def attention_forward(queries, keys_rot, values, segment_row):
    segment_length, heads_here, head_size = queries.shape
    block_rows = min(512, segment_length)
    block_count = segment_length // block_rows
    col_ids = jnp.arange(segment_length, dtype=jnp.int32)

    def one_block(packed):
        query_block, seg_block, row_ids = packed
        scores = score_block(query_block, keys_rot, seg_block, row_ids, segment_row, col_ids)
        row_max = lax.optimization_barrier(jnp.max(scores, -1, keepdims=True))
        log_total = row_max[..., 0] + jnp.log(lax.optimization_barrier(jnp.sum(jnp.exp(scores - row_max), -1)))
        probability = jnp.exp(scores - log_total[..., None]).astype(jnp.bfloat16)
        attended = jnp.einsum('hij,jhd->ihd', probability.astype(jnp.float32), values.astype(jnp.float32)).astype(jnp.bfloat16)
        return (attended, log_total)
    attended, log_totals = lax.map(one_block, (queries.reshape(block_count, block_rows, heads_here, head_size), segment_row.reshape(block_count, block_rows), col_ids.reshape(block_count, block_rows)))
    return (attended.reshape(segment_length, heads_here, head_size), log_totals)

def attention_backward(queries, keys_rot, values, attended, log_totals, grad_att, segment_row):
    segment_length, heads_here, head_size = queries.shape
    block_rows = min(512, segment_length)
    block_count = segment_length // block_rows
    col_ids = jnp.arange(segment_length, dtype=jnp.int32)
    scale = HEAD_DIM ** (-0.5)

    def one_block(running, packed):
        grad_keys, grad_values = running
        query_block, out_block, grad_block, log_total, seg_block, row_ids = packed
        scores = score_block(query_block, keys_rot, seg_block, row_ids, segment_row, col_ids)
        probability = jnp.exp(scores - log_total[..., None])
        prob_low = probability.astype(jnp.bfloat16)
        delta = lax.optimization_barrier(jnp.sum(grad_block.astype(jnp.float32) * out_block.astype(jnp.float32), -1)).T
        grad_values = grad_values + jnp.einsum('hij,ihd->jhd', prob_low.astype(jnp.float32), grad_block.astype(jnp.float32))
        grad_prob = jnp.einsum('ihd,jhd->hij', grad_block.astype(jnp.float32), values.astype(jnp.float32))
        grad_scores = (probability * (grad_prob - delta[..., None]) * scale).astype(jnp.bfloat16).astype(jnp.float32)
        grad_query = jnp.einsum('hij,jhd->ihd', grad_scores, keys_rot.astype(jnp.float32))
        grad_keys = grad_keys + jnp.einsum('hij,ihd->jhd', grad_scores, query_block.astype(jnp.float32))
        return ((grad_keys, grad_values), grad_query)
    zero_field = jnp.zeros((segment_length, heads_here, head_size), jnp.float32)
    shaped = (queries.reshape(block_count, block_rows, heads_here, head_size), attended.reshape(block_count, block_rows, heads_here, head_size), grad_att.reshape(block_count, block_rows, heads_here, head_size), log_totals, segment_row.reshape(block_count, block_rows), col_ids.reshape(block_count, block_rows))
    (grad_keys, grad_values), grad_query = lax.scan(one_block, (zero_field, zero_field), shaped)
    return (grad_query.reshape(segment_length, heads_here, head_size), grad_keys, grad_values)

def reference(hidden_in, cotangent, segments, shared_params, split_params, shared_m1, split_m1, shared_m2, split_m2):
    b_qkv, b_dense, b_proj, gain_one, shift_one, gain_two, shift_two = unpack_shared(shared_params)
    w_qkv, dense_weight, expand_weight, b_fc, contract_weight = unpack_split(split_params.astype(jnp.bfloat16), N_SEQ)
    b_fc = b_fc.astype(jnp.float32)

    def group_pass(running, packed):
        group_in, group_cot, segment_row = packed
        segment_length = group_in.shape[0]
        resid = group_in.astype(jnp.float32)
        first_norm, normed_one, root_one = layer_norm(resid, gain_one, shift_one)
        second_norm, normed_two, root_two = layer_norm(resid, gain_two, shift_two)
        first_low = first_norm.astype(jnp.bfloat16)
        second_low = second_norm.astype(jnp.bfloat16)
        qkv = (jnp.dot(first_low, w_qkv, preferred_element_type=jnp.float32) + b_qkv).astype(jnp.bfloat16).reshape(segment_length, HEADS, 3 * HEAD_DIM)
        cosines, sines = rotary_tables(segment_row)
        queries = rotate(qkv[..., :HEAD_DIM].astype(jnp.float32), cosines, sines, 1.0).astype(jnp.bfloat16)
        keys_rot = rotate(qkv[..., HEAD_DIM:2 * HEAD_DIM].astype(jnp.float32), cosines, sines, 1.0).astype(jnp.bfloat16)
        values = qkv[..., 2 * HEAD_DIM:]
        attended, log_totals = attention_forward(queries, keys_rot, values, segment_row)
        attention_out_rows = attended.reshape(segment_length, MODEL_WIDTH)
        hidden_pre = jnp.dot(second_low, expand_weight, preferred_element_type=jnp.float32) + b_fc
        hidden_activations = jax.nn.gelu(hidden_pre, approximate=False).astype(jnp.bfloat16)
        branch_total = jnp.dot(attention_out_rows, dense_weight, preferred_element_type=jnp.float32) + jnp.dot(hidden_activations, contract_weight, preferred_element_type=jnp.float32)
        total = resid + branch_total + b_dense + b_proj
        output = total.astype(jnp.bfloat16)
        grad_out = group_cot
        grad_outf = grad_out.astype(jnp.float32)
        grad_b_proj = lax.optimization_barrier(jnp.sum(grad_outf, 0))
        grad_b_dense = lax.optimization_barrier(jnp.sum(grad_outf, 0))
        grad_w_proj = jnp.dot(hidden_activations.T, grad_out, preferred_element_type=jnp.float32)
        grad_hidden = jnp.dot(grad_out, contract_weight.T, preferred_element_type=jnp.float32) * gelu_slope(hidden_pre)
        grad_b_fc = lax.optimization_barrier(jnp.sum(grad_hidden, 0))
        hidden_reduced_precision = grad_hidden.astype(jnp.bfloat16)
        grad_w_fc = jnp.dot(second_low.T, hidden_reduced_precision, preferred_element_type=jnp.float32)
        grad_second = jnp.dot(hidden_reduced_precision, expand_weight.T, preferred_element_type=jnp.float32)
        grad_w_dense = jnp.dot(attention_out_rows.T, grad_out, preferred_element_type=jnp.float32)
        grad_att = jnp.dot(grad_out, dense_weight.T, preferred_element_type=jnp.float32).astype(jnp.bfloat16).reshape(segment_length, HEADS, HEAD_DIM)
        grad_query, grad_keys, grad_values = attention_backward(queries, keys_rot, values, attended, log_totals, grad_att, segment_row)
        grad_query = rotate(grad_query, cosines, sines, -1.0)
        grad_keys = rotate(grad_keys, cosines, sines, -1.0)
        grad_qkv = jnp.concatenate([grad_query, grad_keys, grad_values], -1).astype(jnp.bfloat16).reshape(segment_length, 3 * MODEL_WIDTH)
        grad_b_qkv = lax.optimization_barrier(jnp.sum(grad_qkv.astype(jnp.float32), 0))
        grad_w_qkv = jnp.dot(first_low.T, grad_qkv, preferred_element_type=jnp.float32)
        grad_first = jnp.dot(grad_qkv, w_qkv.T, preferred_element_type=jnp.float32)
        grad_gain_one = lax.optimization_barrier(jnp.sum(grad_first * normed_one, 0))
        grad_shift_one = lax.optimization_barrier(jnp.sum(grad_first, 0))
        grad_gain_two = lax.optimization_barrier(jnp.sum(grad_second * normed_two, 0))
        grad_shift_two = lax.optimization_barrier(jnp.sum(grad_second, 0))
        input_grad = grad_outf + norm_back(grad_first, gain_one, normed_one, root_one) + norm_back(grad_second, gain_two, normed_two, root_two)
        shared_flat = jnp.concatenate([grad_b_qkv, grad_b_dense, grad_b_proj, grad_gain_one, grad_shift_one, grad_gain_two, grad_shift_two])
        split_group = pack_split(grad_w_qkv, grad_w_dense, grad_w_fc, grad_b_fc, grad_w_proj, N_SEQ)
        new_running = (running[0] + shared_flat, running[1] + split_group)
        return (new_running, (output, input_grad))
    start = (jnp.zeros((SHARED,), jnp.float32), jnp.zeros((N_SEQ, SPLIT), jnp.float32))
    shaped = (hidden_in.reshape(N_DP, GROUP, MODEL_WIDTH), cotangent.reshape(N_DP, GROUP, MODEL_WIDTH), segments)
    sums, (outputs, input_grads) = lax.scan(group_pass, start, shaped)
    shared_grads = sums[0]
    split_grads = sums[1]
    shared_new, shared_m1_new, shared_m2_new = adamw(shared_params, shared_m1, shared_m2, shared_grads)
    split_new, split_m1_new, split_m2_new = adamw(split_params, split_m1, split_m2, split_grads)
    return (outputs.reshape(TOKENS, MODEL_WIDTH), input_grads.reshape(TOKENS, MODEL_WIDTH), shared_grads, split_grads, shared_new, split_new, shared_m1_new, split_m1_new, shared_m2_new, split_m2_new)
```

```python
import math

import jax
import jax.numpy as jnp
from jax import lax
from jax.sharding import PartitionSpec as P

MODEL_WIDTH = 1024
HEADS = 16
HEAD_DIM = 64
FF = 4096
ROT = 16
STEP = 3


norm_eps = 1e-05
beta_first = 0.9
beta_second = 0.95
adam_eps = 1e-08
learn_rate = 0.1
weight_decay = 0.01
rotary_base = 10000.0
masked_score = -1e30


def unpack_shared(flat_vec):
    extents = [
        (3 * MODEL_WIDTH,),
        (MODEL_WIDTH,),
        (MODEL_WIDTH,),
        (MODEL_WIDTH,),
        (MODEL_WIDTH,),
        (MODEL_WIDTH,),
        (MODEL_WIDTH,),
    ]
    pieces = []
    offset = 0
    for extent in extents:
        number = math.prod(extent)
        pieces.append(flat_vec[offset : offset + number])
        offset = offset + number
    return pieces


def unpack_split(matrix, seq_count):
    rows = matrix.shape[0]
    qkv_part = 3 * MODEL_WIDTH // seq_count
    dense_output_slice = MODEL_WIDTH // seq_count
    hidden_units_slice = FF // seq_count
    zero_end = MODEL_WIDTH * qkv_part
    first_end = zero_end + dense_output_slice * MODEL_WIDTH
    second_end = first_end + MODEL_WIDTH * hidden_units_slice
    third_end = second_end + hidden_units_slice
    w_qkv = (
        matrix[:, :zero_end]
        .reshape(rows, MODEL_WIDTH, qkv_part)
        .transpose(1, 0, 2)
        .reshape(MODEL_WIDTH, rows * qkv_part)
    )
    dense_weight = matrix[:, zero_end:first_end].reshape(rows * dense_output_slice, MODEL_WIDTH)
    expand_weight = (
        matrix[:, first_end:second_end]
        .reshape(rows, MODEL_WIDTH, hidden_units_slice)
        .transpose(1, 0, 2)
        .reshape(MODEL_WIDTH, rows * hidden_units_slice)
    )
    b_fc = matrix[:, second_end:third_end].reshape(rows * hidden_units_slice)
    contract_weight = matrix[:, third_end:].reshape(rows * hidden_units_slice, MODEL_WIDTH)
    return (w_qkv, dense_weight, expand_weight, b_fc, contract_weight)


def pack_split(w_qkv, dense_weight, expand_weight, b_fc, contract_weight, seq_count):
    qkv_part = 3 * MODEL_WIDTH // seq_count
    dense_output_slice = MODEL_WIDTH // seq_count
    hidden_units_slice = FF // seq_count
    rows = dense_weight.shape[0] // dense_output_slice
    return jnp.concatenate(
        [
            w_qkv.reshape(MODEL_WIDTH, rows, qkv_part)
            .transpose(1, 0, 2)
            .reshape(rows, MODEL_WIDTH * qkv_part),
            dense_weight.reshape(rows, dense_output_slice * MODEL_WIDTH),
            expand_weight.reshape(MODEL_WIDTH, rows, hidden_units_slice)
            .transpose(1, 0, 2)
            .reshape(rows, MODEL_WIDTH * hidden_units_slice),
            b_fc.reshape(rows, hidden_units_slice),
            contract_weight.reshape(rows, hidden_units_slice * MODEL_WIDTH),
        ],
        1,
    )


def adamw(param_vals, first_m, second_m, grad_vals):
    first_new = beta_first * first_m + (1.0 - beta_first) * grad_vals
    second_new = beta_second * second_m + (1.0 - beta_second) * grad_vals * grad_vals
    first_hat = first_new / (1.0 - beta_first**STEP)
    second_hat = second_new / (1.0 - beta_second**STEP)
    param_new = param_vals - learn_rate * (
        first_hat / (jnp.sqrt(second_hat) + adam_eps) + weight_decay * param_vals
    )
    return (param_new, first_new, second_new)


def layer_norm(resid, gain_vec, shift_vec):
    average = jnp.mean(resid, -1, keepdims=True)
    centered = resid - average
    variance = jnp.mean(centered * centered, -1, keepdims=True)
    recip_root = lax.rsqrt(variance + norm_eps)
    normed = centered * recip_root
    return (normed * gain_vec + shift_vec, normed, recip_root)


def norm_back(grad_norm, gain_vec, normed, recip_root):
    scaled = grad_norm * gain_vec
    return recip_root * (
        scaled
        - jnp.mean(scaled, -1, keepdims=True)
        - normed * jnp.mean(scaled * normed, -1, keepdims=True)
    )


def gelu_slope(inputs):
    normal_cdf = 0.5 * (1.0 + jax.scipy.special.erf(inputs * 0.7071067811865476))
    return normal_cdf + inputs * jnp.exp(-0.5 * inputs * inputs) * 0.3989422804014327


def rotary_tables(segment_row):
    indices = jnp.arange(segment_row.shape[0], dtype=jnp.int32)
    change = jnp.concatenate([jnp.ones((1,), dtype=jnp.bool_), segment_row[1:] != segment_row[:-1]])
    starts = lax.cummax(jnp.where(change, indices, jnp.zeros_like(indices)), axis=0)
    positions = (indices - starts).astype(jnp.float32)
    frequency = rotary_base ** (-jnp.arange(0, ROT, 2, dtype=jnp.float32) / ROT)
    angles = positions[:, None] * frequency[None, :]
    return (jnp.cos(angles)[:, None, :], jnp.sin(angles)[:, None, :])


def rotate(field, cosines, sines, direction):
    half_rot = ROT // 2
    first_half = field[..., :half_rot]
    second = field[..., half_rot:ROT]
    return jnp.concatenate(
        [
            first_half * cosines - direction * second * sines,
            second * cosines + direction * first_half * sines,
            field[..., ROT:],
        ],
        -1,
    )


def score_block(query_block, keys_rot, seg_block, row_ids, segment_row, col_ids):
    scale = HEAD_DIM ** (-0.5)
    scores = (
        jnp.einsum("ihd,jhd->hij", query_block, keys_rot, preferred_element_type=jnp.float32)
        * scale
    )
    allowed = (seg_block[:, None] == segment_row[None, :]) & (row_ids[:, None] >= col_ids[None, :])
    return jnp.where(allowed[None], scores, masked_score)


def attention_forward(queries, keys_rot, values, segment_row):
    segment_length, heads_here, head_size = queries.shape
    block_rows = min(512, segment_length)
    block_count = segment_length // block_rows
    col_ids = jnp.arange(segment_length, dtype=jnp.int32)

    def one_block(packed):
        query_block, seg_block, row_ids = packed
        scores = score_block(query_block, keys_rot, seg_block, row_ids, segment_row, col_ids)
        row_max = jnp.max(scores, -1, keepdims=True)
        log_total = row_max[..., 0] + jnp.log(jnp.sum(jnp.exp(scores - row_max), -1))
        probability = jnp.exp(scores - log_total[..., None]).astype(jnp.bfloat16)
        attended = jnp.einsum(
            "hij,jhd->ihd", probability, values, preferred_element_type=jnp.float32
        ).astype(jnp.bfloat16)
        return (attended, log_total)

    attended, log_totals = lax.map(
        one_block,
        (
            queries.reshape(block_count, block_rows, heads_here, head_size),
            segment_row.reshape(block_count, block_rows),
            col_ids.reshape(block_count, block_rows),
        ),
    )
    return (attended.reshape(segment_length, heads_here, head_size), log_totals)


def attention_backward(queries, keys_rot, values, attended, log_totals, grad_att, segment_row):
    segment_length, heads_here, head_size = queries.shape
    block_rows = min(512, segment_length)
    block_count = segment_length // block_rows
    col_ids = jnp.arange(segment_length, dtype=jnp.int32)
    scale = HEAD_DIM ** (-0.5)

    def one_block(running, packed):
        grad_keys, grad_values = running
        query_block, out_block, grad_block, log_total, seg_block, row_ids = packed
        scores = score_block(query_block, keys_rot, seg_block, row_ids, segment_row, col_ids)
        probability = jnp.exp(scores - log_total[..., None])
        prob_low = probability.astype(jnp.bfloat16)
        delta = jnp.sum(grad_block.astype(jnp.float32) * out_block.astype(jnp.float32), -1).T
        grad_values = grad_values + jnp.einsum(
            "hij,ihd->jhd", prob_low, grad_block, preferred_element_type=jnp.float32
        )
        grad_prob = jnp.einsum(
            "ihd,jhd->hij", grad_block, values, preferred_element_type=jnp.float32
        )
        grad_scores = (probability * (grad_prob - delta[..., None]) * scale).astype(jnp.bfloat16)
        grad_query = jnp.einsum(
            "hij,jhd->ihd", grad_scores, keys_rot, preferred_element_type=jnp.float32
        )
        grad_keys = grad_keys + jnp.einsum(
            "hij,ihd->jhd", grad_scores, query_block, preferred_element_type=jnp.float32
        )
        return ((grad_keys, grad_values), grad_query)

    zero_field = jnp.zeros((segment_length, heads_here, head_size), jnp.float32)
    shaped = (
        queries.reshape(block_count, block_rows, heads_here, head_size),
        attended.reshape(block_count, block_rows, heads_here, head_size),
        grad_att.reshape(block_count, block_rows, heads_here, head_size),
        log_totals,
        segment_row.reshape(block_count, block_rows),
        col_ids.reshape(block_count, block_rows),
    )
    (grad_keys, grad_values), grad_query = lax.scan(one_block, (zero_field, zero_field), shaped)
    return (grad_query.reshape(segment_length, heads_here, head_size), grad_keys, grad_values)


def local_general(
    hidden_in,
    cotangent,
    segments,
    shared_params,
    split_params,
    shared_m1,
    split_m1,
    shared_m2,
    split_m2,
):
    tokens_here = hidden_in.shape[0]
    seq_count = lax.axis_size("seq")
    heads_here = HEADS // seq_count
    qkv_cols = 3 * MODEL_WIDTH // seq_count
    shared_full = lax.all_gather(shared_params, ("dp", "seq"), axis=0, tiled=True)
    b_qkv, b_dense, b_proj, gain_one, shift_one, gain_two, shift_two = unpack_shared(shared_full)
    split_mine = lax.all_gather(split_params.astype(jnp.bfloat16), "dp", axis=1, tiled=True)
    w_qkv_share, dense_weight, expand_weight, b_fc, contract_weight = unpack_split(
        split_mine, seq_count
    )
    b_fc = b_fc.astype(jnp.float32)
    column_rows = lax.all_gather(split_mine[:, : MODEL_WIDTH * qkv_cols], "seq", axis=0, tiled=True)
    w_qkv = (
        column_rows.reshape(seq_count, MODEL_WIDTH, qkv_cols)
        .transpose(1, 0, 2)
        .reshape(MODEL_WIDTH, 3 * MODEL_WIDTH)
    )
    resid = hidden_in.astype(jnp.float32)
    first_norm, normed_one, root_one = layer_norm(resid, gain_one, shift_one)
    second_norm, normed_two, root_two = layer_norm(resid, gain_two, shift_two)
    first_low = first_norm.astype(jnp.bfloat16)
    second_low = second_norm.astype(jnp.bfloat16)
    group_first, group_norm, group_cot = (
        lax.all_gather(first_low, "seq", axis=0, tiled=True),
        lax.all_gather(second_low, "seq", axis=0, tiled=True),
        lax.all_gather(cotangent, "seq", axis=0, tiled=True),
    )
    group_length = group_first.shape[0]
    qkv = (
        (jnp.dot(first_low, w_qkv, preferred_element_type=jnp.float32) + b_qkv)
        .astype(jnp.bfloat16)
        .reshape(tokens_here, HEADS, 3 * HEAD_DIM)
    )
    grouped = lax.all_to_all(qkv, "seq", split_axis=1, concat_axis=0, tiled=True)
    segment_row = segments[0]
    cosines, sines = rotary_tables(segment_row)
    queries = rotate(grouped[..., :HEAD_DIM].astype(jnp.float32), cosines, sines, 1.0).astype(
        jnp.bfloat16
    )
    keys_rot = rotate(
        grouped[..., HEAD_DIM : 2 * HEAD_DIM].astype(jnp.float32), cosines, sines, 1.0
    ).astype(jnp.bfloat16)
    values = grouped[..., 2 * HEAD_DIM :]
    attended, log_totals = attention_forward(queries, keys_rot, values, segment_row)
    grad_outf = cotangent.astype(jnp.float32)
    grad_b_proj = jnp.sum(grad_outf, 0)
    grad_b_dense = jnp.sum(grad_outf, 0)
    att_flat = attended.reshape(group_length, heads_here * HEAD_DIM)
    hidden_pre = jnp.dot(group_norm, expand_weight, preferred_element_type=jnp.float32) + b_fc
    hidden_activations = jax.nn.gelu(hidden_pre, approximate=False).astype(jnp.bfloat16)
    branch = jnp.dot(att_flat, dense_weight, preferred_element_type=jnp.float32) + jnp.dot(
        hidden_activations, contract_weight, preferred_element_type=jnp.float32
    )
    total = (
        resid + lax.psum_scatter(branch, "seq", scatter_dimension=0, tiled=True) + b_dense + b_proj
    )
    output = total.astype(jnp.bfloat16)
    grad_w_proj = jnp.dot(hidden_activations.T, group_cot, preferred_element_type=jnp.float32)
    grad_hidden = jnp.dot(
        group_cot, contract_weight.T, preferred_element_type=jnp.float32
    ) * gelu_slope(hidden_pre)
    grad_b_fc = jnp.sum(grad_hidden, 0)
    hidden_reduced_precision = grad_hidden.astype(jnp.bfloat16)
    grad_w_fc = jnp.dot(group_norm.T, hidden_reduced_precision, preferred_element_type=jnp.float32)
    grad_second = lax.psum_scatter(
        jnp.dot(hidden_reduced_precision, expand_weight.T, preferred_element_type=jnp.float32),
        "seq",
        scatter_dimension=0,
        tiled=True,
    )
    grad_w_dense = jnp.dot(att_flat.T, group_cot, preferred_element_type=jnp.float32)
    grad_att_heads = (
        jnp.dot(group_cot, dense_weight.T, preferred_element_type=jnp.float32)
        .astype(jnp.bfloat16)
        .reshape(group_length, heads_here, HEAD_DIM)
    )
    grad_query, grad_keys, grad_values = attention_backward(
        queries, keys_rot, values, attended, log_totals, grad_att_heads, segment_row
    )
    grad_query = rotate(grad_query, cosines, sines, -1.0)
    grad_keys = rotate(grad_keys, cosines, sines, -1.0)
    grad_grouped = jnp.concatenate([grad_query, grad_keys, grad_values], -1).astype(jnp.bfloat16)
    grad_w_qkv_share = jnp.dot(
        group_first.T,
        grad_grouped.reshape(group_length, qkv_cols),
        preferred_element_type=jnp.float32,
    )
    grad_qkv = lax.all_to_all(grad_grouped, "seq", split_axis=0, concat_axis=1, tiled=True).reshape(
        tokens_here, 3 * MODEL_WIDTH
    )
    grad_b_qkv = jnp.sum(grad_qkv.astype(jnp.float32), 0)
    grad_first = jnp.dot(grad_qkv, w_qkv.T, preferred_element_type=jnp.float32)
    grad_gain_one = jnp.sum(grad_first * normed_one, 0)
    grad_shift_one = jnp.sum(grad_first, 0)
    grad_gain_two = jnp.sum(grad_second * normed_two, 0)
    grad_shift_two = jnp.sum(grad_second, 0)
    input_grad = (
        grad_outf
        + norm_back(grad_first, gain_one, normed_one, root_one)
        + norm_back(grad_second, gain_two, normed_two, root_two)
    )
    shared_flat = jnp.concatenate(
        [
            grad_b_qkv,
            grad_b_dense,
            grad_b_proj,
            grad_gain_one,
            grad_shift_one,
            grad_gain_two,
            grad_shift_two,
        ]
    )
    shared_grads = lax.psum_scatter(shared_flat, ("dp", "seq"), scatter_dimension=0, tiled=True)
    split_local = pack_split(
        grad_w_qkv_share, grad_w_dense, grad_w_fc, grad_b_fc, grad_w_proj, seq_count
    )
    split_grads = lax.psum_scatter(split_local, "dp", scatter_dimension=1, tiled=True)
    shared_new, shared_m1_new, shared_m2_new = adamw(
        shared_params, shared_m1, shared_m2, shared_grads
    )
    split_new, split_m1_new, split_m2_new = adamw(split_params, split_m1, split_m2, split_grads)
    return (
        output,
        input_grad,
        shared_grads,
        split_grads,
        shared_new,
        split_new,
        shared_m1_new,
        split_m1_new,
        shared_m2_new,
        split_m2_new,
    )


LANES = 128


def share_layout(seq_count):
    ql = 3 * MODEL_WIDTH // seq_count
    dl = MODEL_WIDTH // seq_count
    fl = FF // seq_count
    return [
        MODEL_WIDTH * ql // LANES,
        dl * MODEL_WIDTH // LANES,
        MODEL_WIDTH * fl // LANES,
        fl // LANES,
        fl * MODEL_WIDTH // LANES,
    ]


def gather_parts(split_params, shared_params, dp_count, seq_count):
    rows = split_params.shape[1] // LANES
    mine = split_params.reshape(rows, LANES).astype(jnp.bfloat16)
    mine = jnp.pad(mine, ((0, -rows % 16), (0, 0)))
    blocks = lax.all_gather(mine, "dp", axis=0, tiled=False)
    full = blocks[:, :rows].reshape(dp_count * rows, LANES)
    shared_full = lax.all_gather(shared_params, ("dp", "seq"), axis=0, tiled=True)
    return full, shared_full


def reduce_parts(flat, shared_flat, dp_count, seq_count):
    rows = flat.shape[0] // dp_count
    blocks = flat.reshape(dp_count, rows, LANES)
    got = lax.all_to_all(blocks, "dp", split_axis=0, concat_axis=0, tiled=True)
    grads = jnp.sum(got.astype(jnp.float32), 0).reshape(1, rows * LANES)
    shared = lax.psum_scatter(shared_flat, ("dp", "seq"), scatter_dimension=0, tiled=True)
    return grads, shared


def attend(queries, keys_rot, values, segment_row):
    length = queries.shape[1]
    ids = jnp.arange(length, dtype=jnp.int32)
    allowed = (segment_row[:, None] == segment_row[None, :]) & (ids[:, None] >= ids[None, :])
    scores = jnp.einsum("hid,hjd->hij", queries, keys_rot, preferred_element_type=jnp.float32)
    scores = jnp.where(allowed[None], scores * HEAD_DIM ** (-0.5), masked_score)
    row_max = jnp.max(scores, -1, keepdims=True)
    log_total = row_max + jnp.log(jnp.sum(jnp.exp(scores - row_max), -1, keepdims=True))
    prob = jnp.exp(scores - log_total)
    prob_low = prob.astype(jnp.bfloat16)
    attended = jnp.einsum("hij,hjd->hid", prob_low, values, preferred_element_type=jnp.float32)
    return attended.astype(jnp.bfloat16), prob, prob_low


def attend_back(queries, keys_rot, values, attended, prob, prob_low, grad_att):
    delta = jnp.sum(grad_att.astype(jnp.float32) * attended.astype(jnp.float32), -1, keepdims=True)
    grad_values = jnp.einsum("hij,hid->hjd", prob_low, grad_att, preferred_element_type=jnp.float32)
    grad_prob = jnp.einsum("hid,hjd->hij", grad_att, values, preferred_element_type=jnp.float32)
    grad_scores = (prob * (grad_prob - delta) * HEAD_DIM ** (-0.5)).astype(jnp.bfloat16)
    grad_query = jnp.einsum(
        "hij,hjd->hid", grad_scores, keys_rot, preferred_element_type=jnp.float32
    )
    grad_keys = jnp.einsum("hij,hid->hjd", grad_scores, queries, preferred_element_type=jnp.float32)
    return grad_query, grad_keys, grad_values


def local_grouped(
    hidden_in,
    cotangent,
    segments,
    shared_params,
    split_params,
    shared_m1,
    split_m1,
    shared_m2,
    split_m2,
):
    dp_count = lax.axis_size("dp")
    seq_count = lax.axis_size("seq")
    share = lax.axis_index("seq")
    heads_here = HEADS // seq_count
    ql = 3 * MODEL_WIDTH // seq_count
    dl = MODEL_WIDTH // seq_count
    fl = FF // seq_count
    f32, bf16 = jnp.float32, jnp.bfloat16
    tokens_here = hidden_in.shape[0]
    both = lax.all_gather(
        jnp.concatenate([hidden_in, cotangent], 1), "seq", axis=0, tiled=True
    )
    group_hidden, group_cot = both[:, :MODEL_WIDTH], both[:, MODEL_WIDTH:]
    full, shared_full = gather_parts(split_params, shared_params, dp_count, seq_count)
    b_qkv, b_dense, b_proj, gain_one, shift_one, gain_two, shift_two = unpack_shared(shared_full)
    extents = share_layout(seq_count)
    offsets = [sum(extents[:k]) for k in range(6)]
    w_qkv, w_dense, w_fc, b_fc, w_proj = [
        full[offsets[k] : offsets[k + 1]].reshape(shape)
        for k, shape in enumerate(
            [(MODEL_WIDTH, ql), (dl, MODEL_WIDTH), (MODEL_WIDTH, fl), (fl,), (fl, MODEL_WIDTH)]
        )
    ]
    b_fc = b_fc.astype(f32)
    b_qkv_mine = lax.dynamic_slice(b_qkv, (share * ql,), (ql,))

    resid = group_hidden.astype(f32)
    first_norm, normed, root = layer_norm(resid, gain_one, shift_one)
    first_low = first_norm.astype(bf16)
    second_low = (normed * gain_two + shift_two).astype(bf16)
    length = resid.shape[0]

    qkv = (jnp.dot(first_low, w_qkv, preferred_element_type=f32) + b_qkv_mine).astype(bf16)
    qkv = qkv.reshape(length, heads_here, 3, HEAD_DIM).transpose(2, 1, 0, 3)
    segment_row = segments[0]
    cosines, sines = rotary_tables(segment_row)
    cosines, sines = cosines[:, 0], sines[:, 0]
    queries = rotate(qkv[0].astype(f32), cosines, sines, 1.0).astype(bf16)
    keys_rot = rotate(qkv[1].astype(f32), cosines, sines, 1.0).astype(bf16)
    values = qkv[2]
    attended, prob, prob_low = attend(queries, keys_rot, values, segment_row)
    att_flat = attended.transpose(1, 0, 2).reshape(length, dl)

    hidden_pre = jnp.dot(second_low, w_fc, preferred_element_type=f32) + b_fc
    activated = jax.nn.gelu(hidden_pre, approximate=False).astype(bf16)
    branch = jnp.dot(att_flat, w_dense, preferred_element_type=f32) + jnp.dot(
        activated, w_proj, preferred_element_type=f32
    )
    total = lax.psum_scatter(branch, "seq", scatter_dimension=0, tiled=True)
    output = (hidden_in.astype(f32) + total + b_dense + b_proj).astype(bf16)

    grad_outf = cotangent.astype(f32)
    grad_b_out = jnp.sum(grad_outf, 0)
    grad_w_proj = jnp.dot(activated.T, group_cot, preferred_element_type=f32)
    grad_hidden = jnp.dot(group_cot, w_proj.T, preferred_element_type=f32) * gelu_slope(hidden_pre)
    grad_b_fc = jnp.sum(grad_hidden, 0)
    grad_hidden_low = grad_hidden.astype(bf16)
    grad_w_fc = jnp.dot(second_low.T, grad_hidden_low, preferred_element_type=f32)
    grad_second = jnp.dot(grad_hidden_low, w_fc.T, preferred_element_type=f32)
    grad_w_dense = jnp.dot(att_flat.T, group_cot, preferred_element_type=f32)
    grad_att = (
        jnp.dot(group_cot, w_dense.T, preferred_element_type=f32)
        .astype(bf16)
        .reshape(length, heads_here, HEAD_DIM)
        .transpose(1, 0, 2)
    )
    grad_query, grad_keys, grad_values = attend_back(
        queries, keys_rot, values, attended, prob, prob_low, grad_att
    )
    grad_query = rotate(grad_query, cosines, sines, -1.0)
    grad_keys = rotate(grad_keys, cosines, sines, -1.0)
    grad_qkv = (
        jnp.stack([grad_query, grad_keys, grad_values])
        .astype(bf16)
        .transpose(2, 1, 0, 3)
        .reshape(length, ql)
    )
    grad_b_qkv = jnp.sum(grad_qkv.astype(f32), 0)
    grad_w_qkv = jnp.dot(first_low.T, grad_qkv, preferred_element_type=f32)
    grad_first = jnp.dot(grad_qkv, w_qkv.T, preferred_element_type=f32)

    scaled = lax.psum_scatter(
        gain_one * grad_first + gain_two * grad_second, "seq", scatter_dimension=0, tiled=True
    )
    normed_mine = lax.dynamic_slice(normed, (share * tokens_here, 0), (tokens_here, MODEL_WIDTH))
    root_mine = lax.dynamic_slice(root, (share * tokens_here, 0), (tokens_here, 1))
    input_grad = grad_outf + norm_back(scaled, 1.0, normed_mine, root_mine)

    shared_flat = jnp.concatenate(
        [
            lax.dynamic_update_slice(
                jnp.zeros((3 * MODEL_WIDTH,), f32), grad_b_qkv, (share * ql,)
            ),
            grad_b_out,
            grad_b_out,
            jnp.sum(grad_first * normed, 0),
            jnp.sum(grad_first, 0),
            jnp.sum(grad_second * normed, 0),
            jnp.sum(grad_second, 0),
        ]
    )
    flat = jnp.concatenate(
        [
            part.astype(bf16).reshape(-1, LANES)
            for part in (grad_w_qkv, grad_w_dense, grad_w_fc, grad_b_fc, grad_w_proj)
        ]
    )
    split_grads, shared_grads = reduce_parts(flat, shared_flat, dp_count, seq_count)
    shared_new, shared_m1_new, shared_m2_new = adamw(
        shared_params, shared_m1, shared_m2, shared_grads
    )
    split_new, split_m1_new, split_m2_new = adamw(split_params, split_m1, split_m2, split_grads)
    return (
        output,
        input_grad,
        shared_grads,
        split_grads,
        shared_new,
        split_new,
        shared_m1_new,
        split_m1_new,
        shared_m2_new,
        split_m2_new,
    )


def solution(mesh):
    in_specs = (
        P(("dp", "seq"), None),
        P(("dp", "seq"), None),
        P("dp", None),
        P(("dp", "seq")),
        P("seq", "dp"),
        P(("dp", "seq")),
        P("seq", "dp"),
        P(("dp", "seq")),
        P("seq", "dp"),
    )
    out_specs = (
        P(("dp", "seq"), None),
        P(("dp", "seq"), None),
        P(("dp", "seq")),
        P("seq", "dp"),
        P(("dp", "seq")),
        P("seq", "dp"),
        P(("dp", "seq")),
        P("seq", "dp"),
        P(("dp", "seq")),
        P("seq", "dp"),
    )
    dp_count, seq_count = mesh.shape["dp"], mesh.shape["seq"]
    even = sum(share_layout(seq_count)) % dp_count == 0
    local = local_grouped if even else local_general
    return jax.shard_map(local, mesh=mesh, in_specs=in_specs, out_specs=out_specs, check_vma=False)
```

```python
import math

import jax
import jax.numpy as jnp
from jax import lax
from jax.experimental import pallas as pl
from jax.experimental.pallas import tpu as pltpu
from jax.sharding import PartitionSpec as P

MODEL_WIDTH = 1024
HEADS = 16
HEAD_DIM = 64
FF = 4096
ROT = 16
STEP = 3


norm_eps = 1e-05
beta_first = 0.9
beta_second = 0.95
adam_eps = 1e-08
learn_rate = 0.1
weight_decay = 0.01
rotary_base = 10000.0
masked_score = -1e30


def unpack_shared(flat_vec):
    extents = [
        (3 * MODEL_WIDTH,),
        (MODEL_WIDTH,),
        (MODEL_WIDTH,),
        (MODEL_WIDTH,),
        (MODEL_WIDTH,),
        (MODEL_WIDTH,),
        (MODEL_WIDTH,),
    ]
    pieces = []
    offset = 0
    for extent in extents:
        number = math.prod(extent)
        pieces.append(flat_vec[offset : offset + number])
        offset = offset + number
    return pieces


def unpack_split(matrix, seq_count):
    rows = matrix.shape[0]
    qkv_part = 3 * MODEL_WIDTH // seq_count
    dense_output_slice = MODEL_WIDTH // seq_count
    hidden_units_slice = FF // seq_count
    zero_end = MODEL_WIDTH * qkv_part
    first_end = zero_end + dense_output_slice * MODEL_WIDTH
    second_end = first_end + MODEL_WIDTH * hidden_units_slice
    third_end = second_end + hidden_units_slice
    w_qkv = (
        matrix[:, :zero_end]
        .reshape(rows, MODEL_WIDTH, qkv_part)
        .transpose(1, 0, 2)
        .reshape(MODEL_WIDTH, rows * qkv_part)
    )
    dense_weight = matrix[:, zero_end:first_end].reshape(rows * dense_output_slice, MODEL_WIDTH)
    expand_weight = (
        matrix[:, first_end:second_end]
        .reshape(rows, MODEL_WIDTH, hidden_units_slice)
        .transpose(1, 0, 2)
        .reshape(MODEL_WIDTH, rows * hidden_units_slice)
    )
    b_fc = matrix[:, second_end:third_end].reshape(rows * hidden_units_slice)
    contract_weight = matrix[:, third_end:].reshape(rows * hidden_units_slice, MODEL_WIDTH)
    return (w_qkv, dense_weight, expand_weight, b_fc, contract_weight)


def pack_split(w_qkv, dense_weight, expand_weight, b_fc, contract_weight, seq_count):
    qkv_part = 3 * MODEL_WIDTH // seq_count
    dense_output_slice = MODEL_WIDTH // seq_count
    hidden_units_slice = FF // seq_count
    rows = dense_weight.shape[0] // dense_output_slice
    return jnp.concatenate(
        [
            w_qkv.reshape(MODEL_WIDTH, rows, qkv_part)
            .transpose(1, 0, 2)
            .reshape(rows, MODEL_WIDTH * qkv_part),
            dense_weight.reshape(rows, dense_output_slice * MODEL_WIDTH),
            expand_weight.reshape(MODEL_WIDTH, rows, hidden_units_slice)
            .transpose(1, 0, 2)
            .reshape(rows, MODEL_WIDTH * hidden_units_slice),
            b_fc.reshape(rows, hidden_units_slice),
            contract_weight.reshape(rows, hidden_units_slice * MODEL_WIDTH),
        ],
        1,
    )


def adamw(param_vals, first_m, second_m, grad_vals):
    first_new = beta_first * first_m + (1.0 - beta_first) * grad_vals
    second_new = beta_second * second_m + (1.0 - beta_second) * grad_vals * grad_vals
    first_hat = first_new / (1.0 - beta_first**STEP)
    second_hat = second_new / (1.0 - beta_second**STEP)
    param_new = param_vals - learn_rate * (
        first_hat / (jnp.sqrt(second_hat) + adam_eps) + weight_decay * param_vals
    )
    return (param_new, first_new, second_new)


def layer_norm(resid, gain_vec, shift_vec):
    average = jnp.mean(resid, -1, keepdims=True)
    centered = resid - average
    variance = jnp.mean(centered * centered, -1, keepdims=True)
    recip_root = lax.rsqrt(variance + norm_eps)
    normed = centered * recip_root
    return (normed * gain_vec + shift_vec, normed, recip_root)


def norm_back(grad_norm, gain_vec, normed, recip_root):
    scaled = grad_norm * gain_vec
    return recip_root * (
        scaled
        - jnp.mean(scaled, -1, keepdims=True)
        - normed * jnp.mean(scaled * normed, -1, keepdims=True)
    )


def gelu_slope(inputs):
    normal_cdf = 0.5 * (1.0 + jax.scipy.special.erf(inputs * 0.7071067811865476))
    return normal_cdf + inputs * jnp.exp(-0.5 * inputs * inputs) * 0.3989422804014327


def rotary_tables(segment_row):
    indices = jnp.arange(segment_row.shape[0], dtype=jnp.int32)
    change = jnp.concatenate([jnp.ones((1,), dtype=jnp.bool_), segment_row[1:] != segment_row[:-1]])
    starts = lax.cummax(jnp.where(change, indices, jnp.zeros_like(indices)), axis=0)
    positions = (indices - starts).astype(jnp.float32)
    frequency = rotary_base ** (-jnp.arange(0, ROT, 2, dtype=jnp.float32) / ROT)
    angles = positions[:, None] * frequency[None, :]
    return (jnp.cos(angles)[:, None, :], jnp.sin(angles)[:, None, :])


def rotate(field, cosines, sines, direction):
    half_rot = ROT // 2
    first_half = field[..., :half_rot]
    second = field[..., half_rot:ROT]
    return jnp.concatenate(
        [
            first_half * cosines - direction * second * sines,
            second * cosines + direction * first_half * sines,
            field[..., ROT:],
        ],
        -1,
    )


def score_block(query_block, keys_rot, seg_block, row_ids, segment_row, col_ids):
    scale = HEAD_DIM ** (-0.5)
    scores = (
        jnp.einsum("ihd,jhd->hij", query_block, keys_rot, preferred_element_type=jnp.float32)
        * scale
    )
    allowed = (seg_block[:, None] == segment_row[None, :]) & (row_ids[:, None] >= col_ids[None, :])
    return jnp.where(allowed[None], scores, masked_score)


def attention_forward(queries, keys_rot, values, segment_row):
    segment_length, heads_here, head_size = queries.shape
    block_rows = min(512, segment_length)
    block_count = segment_length // block_rows
    col_ids = jnp.arange(segment_length, dtype=jnp.int32)

    def one_block(packed):
        query_block, seg_block, row_ids = packed
        scores = score_block(query_block, keys_rot, seg_block, row_ids, segment_row, col_ids)
        row_max = jnp.max(scores, -1, keepdims=True)
        log_total = row_max[..., 0] + jnp.log(jnp.sum(jnp.exp(scores - row_max), -1))
        probability = jnp.exp(scores - log_total[..., None]).astype(jnp.bfloat16)
        attended = jnp.einsum(
            "hij,jhd->ihd", probability, values, preferred_element_type=jnp.float32
        ).astype(jnp.bfloat16)
        return (attended, log_total)

    attended, log_totals = lax.map(
        one_block,
        (
            queries.reshape(block_count, block_rows, heads_here, head_size),
            segment_row.reshape(block_count, block_rows),
            col_ids.reshape(block_count, block_rows),
        ),
    )
    return (attended.reshape(segment_length, heads_here, head_size), log_totals)


def attention_backward(queries, keys_rot, values, attended, log_totals, grad_att, segment_row):
    segment_length, heads_here, head_size = queries.shape
    block_rows = min(512, segment_length)
    block_count = segment_length // block_rows
    col_ids = jnp.arange(segment_length, dtype=jnp.int32)
    scale = HEAD_DIM ** (-0.5)

    def one_block(running, packed):
        grad_keys, grad_values = running
        query_block, out_block, grad_block, log_total, seg_block, row_ids = packed
        scores = score_block(query_block, keys_rot, seg_block, row_ids, segment_row, col_ids)
        probability = jnp.exp(scores - log_total[..., None])
        prob_low = probability.astype(jnp.bfloat16)
        delta = jnp.sum(grad_block.astype(jnp.float32) * out_block.astype(jnp.float32), -1).T
        grad_values = grad_values + jnp.einsum(
            "hij,ihd->jhd", prob_low, grad_block, preferred_element_type=jnp.float32
        )
        grad_prob = jnp.einsum(
            "ihd,jhd->hij", grad_block, values, preferred_element_type=jnp.float32
        )
        grad_scores = (probability * (grad_prob - delta[..., None]) * scale).astype(jnp.bfloat16)
        grad_query = jnp.einsum(
            "hij,jhd->ihd", grad_scores, keys_rot, preferred_element_type=jnp.float32
        )
        grad_keys = grad_keys + jnp.einsum(
            "hij,ihd->jhd", grad_scores, query_block, preferred_element_type=jnp.float32
        )
        return ((grad_keys, grad_values), grad_query)

    zero_field = jnp.zeros((segment_length, heads_here, head_size), jnp.float32)
    shaped = (
        queries.reshape(block_count, block_rows, heads_here, head_size),
        attended.reshape(block_count, block_rows, heads_here, head_size),
        grad_att.reshape(block_count, block_rows, heads_here, head_size),
        log_totals,
        segment_row.reshape(block_count, block_rows),
        col_ids.reshape(block_count, block_rows),
    )
    (grad_keys, grad_values), grad_query = lax.scan(one_block, (zero_field, zero_field), shaped)
    return (grad_query.reshape(segment_length, heads_here, head_size), grad_keys, grad_values)


def local_general(
    hidden_in,
    cotangent,
    segments,
    shared_params,
    split_params,
    shared_m1,
    split_m1,
    shared_m2,
    split_m2,
):
    tokens_here = hidden_in.shape[0]
    seq_count = lax.axis_size("seq")
    heads_here = HEADS // seq_count
    qkv_cols = 3 * MODEL_WIDTH // seq_count
    shared_full = lax.all_gather(shared_params, ("dp", "seq"), axis=0, tiled=True)
    b_qkv, b_dense, b_proj, gain_one, shift_one, gain_two, shift_two = unpack_shared(shared_full)
    split_mine = lax.all_gather(split_params.astype(jnp.bfloat16), "dp", axis=1, tiled=True)
    w_qkv_share, dense_weight, expand_weight, b_fc, contract_weight = unpack_split(
        split_mine, seq_count
    )
    b_fc = b_fc.astype(jnp.float32)
    column_rows = lax.all_gather(split_mine[:, : MODEL_WIDTH * qkv_cols], "seq", axis=0, tiled=True)
    w_qkv = (
        column_rows.reshape(seq_count, MODEL_WIDTH, qkv_cols)
        .transpose(1, 0, 2)
        .reshape(MODEL_WIDTH, 3 * MODEL_WIDTH)
    )
    resid = hidden_in.astype(jnp.float32)
    first_norm, normed_one, root_one = layer_norm(resid, gain_one, shift_one)
    second_norm, normed_two, root_two = layer_norm(resid, gain_two, shift_two)
    first_low = first_norm.astype(jnp.bfloat16)
    second_low = second_norm.astype(jnp.bfloat16)
    group_first, group_norm, group_cot = (
        lax.all_gather(first_low, "seq", axis=0, tiled=True),
        lax.all_gather(second_low, "seq", axis=0, tiled=True),
        lax.all_gather(cotangent, "seq", axis=0, tiled=True),
    )
    group_length = group_first.shape[0]
    qkv = (
        (jnp.dot(first_low, w_qkv, preferred_element_type=jnp.float32) + b_qkv)
        .astype(jnp.bfloat16)
        .reshape(tokens_here, HEADS, 3 * HEAD_DIM)
    )
    grouped = lax.all_to_all(qkv, "seq", split_axis=1, concat_axis=0, tiled=True)
    segment_row = segments[0]
    cosines, sines = rotary_tables(segment_row)
    queries = rotate(grouped[..., :HEAD_DIM].astype(jnp.float32), cosines, sines, 1.0).astype(
        jnp.bfloat16
    )
    keys_rot = rotate(
        grouped[..., HEAD_DIM : 2 * HEAD_DIM].astype(jnp.float32), cosines, sines, 1.0
    ).astype(jnp.bfloat16)
    values = grouped[..., 2 * HEAD_DIM :]
    attended, log_totals = attention_forward(queries, keys_rot, values, segment_row)
    grad_outf = cotangent.astype(jnp.float32)
    grad_b_proj = jnp.sum(grad_outf, 0)
    grad_b_dense = jnp.sum(grad_outf, 0)
    att_flat = attended.reshape(group_length, heads_here * HEAD_DIM)
    hidden_pre = jnp.dot(group_norm, expand_weight, preferred_element_type=jnp.float32) + b_fc
    hidden_activations = jax.nn.gelu(hidden_pre, approximate=False).astype(jnp.bfloat16)
    branch = jnp.dot(att_flat, dense_weight, preferred_element_type=jnp.float32) + jnp.dot(
        hidden_activations, contract_weight, preferred_element_type=jnp.float32
    )
    total = (
        resid + lax.psum_scatter(branch, "seq", scatter_dimension=0, tiled=True) + b_dense + b_proj
    )
    output = total.astype(jnp.bfloat16)
    grad_w_proj = jnp.dot(hidden_activations.T, group_cot, preferred_element_type=jnp.float32)
    grad_hidden = jnp.dot(
        group_cot, contract_weight.T, preferred_element_type=jnp.float32
    ) * gelu_slope(hidden_pre)
    grad_b_fc = jnp.sum(grad_hidden, 0)
    hidden_reduced_precision = grad_hidden.astype(jnp.bfloat16)
    grad_w_fc = jnp.dot(group_norm.T, hidden_reduced_precision, preferred_element_type=jnp.float32)
    grad_second = lax.psum_scatter(
        jnp.dot(hidden_reduced_precision, expand_weight.T, preferred_element_type=jnp.float32),
        "seq",
        scatter_dimension=0,
        tiled=True,
    )
    grad_w_dense = jnp.dot(att_flat.T, group_cot, preferred_element_type=jnp.float32)
    grad_att_heads = (
        jnp.dot(group_cot, dense_weight.T, preferred_element_type=jnp.float32)
        .astype(jnp.bfloat16)
        .reshape(group_length, heads_here, HEAD_DIM)
    )
    grad_query, grad_keys, grad_values = attention_backward(
        queries, keys_rot, values, attended, log_totals, grad_att_heads, segment_row
    )
    grad_query = rotate(grad_query, cosines, sines, -1.0)
    grad_keys = rotate(grad_keys, cosines, sines, -1.0)
    grad_grouped = jnp.concatenate([grad_query, grad_keys, grad_values], -1).astype(jnp.bfloat16)
    grad_w_qkv_share = jnp.dot(
        group_first.T,
        grad_grouped.reshape(group_length, qkv_cols),
        preferred_element_type=jnp.float32,
    )
    grad_qkv = lax.all_to_all(grad_grouped, "seq", split_axis=0, concat_axis=1, tiled=True).reshape(
        tokens_here, 3 * MODEL_WIDTH
    )
    grad_b_qkv = jnp.sum(grad_qkv.astype(jnp.float32), 0)
    grad_first = jnp.dot(grad_qkv, w_qkv.T, preferred_element_type=jnp.float32)
    grad_gain_one = jnp.sum(grad_first * normed_one, 0)
    grad_shift_one = jnp.sum(grad_first, 0)
    grad_gain_two = jnp.sum(grad_second * normed_two, 0)
    grad_shift_two = jnp.sum(grad_second, 0)
    input_grad = (
        grad_outf
        + norm_back(grad_first, gain_one, normed_one, root_one)
        + norm_back(grad_second, gain_two, normed_two, root_two)
    )
    shared_flat = jnp.concatenate(
        [
            grad_b_qkv,
            grad_b_dense,
            grad_b_proj,
            grad_gain_one,
            grad_shift_one,
            grad_gain_two,
            grad_shift_two,
        ]
    )
    shared_grads = lax.psum_scatter(shared_flat, ("dp", "seq"), scatter_dimension=0, tiled=True)
    split_local = pack_split(
        grad_w_qkv_share, grad_w_dense, grad_w_fc, grad_b_fc, grad_w_proj, seq_count
    )
    split_grads = lax.psum_scatter(split_local, "dp", scatter_dimension=1, tiled=True)
    shared_new, shared_m1_new, shared_m2_new = adamw(
        shared_params, shared_m1, shared_m2, shared_grads
    )
    split_new, split_m1_new, split_m2_new = adamw(split_params, split_m1, split_m2, split_grads)
    return (
        output,
        input_grad,
        shared_grads,
        split_grads,
        shared_new,
        split_new,
        shared_m1_new,
        split_m1_new,
        shared_m2_new,
        split_m2_new,
    )


LANES = 128


def share_layout(seq_count):
    ql = 3 * MODEL_WIDTH // seq_count
    dl = MODEL_WIDTH // seq_count
    fl = FF // seq_count
    return [
        MODEL_WIDTH * ql // LANES,
        dl * MODEL_WIDTH // LANES,
        MODEL_WIDTH * fl // LANES,
        fl // LANES,
        fl * MODEL_WIDTH // LANES,
    ]


Z = 4
DP = 2 * Z
SEQ = 4
BLOCK = 3072
EDGE = 16
SPAN = BLOCK + EDGE
MESH = pl.DeviceIdType.MESH
GATHER_CHUNKS = [(k * 768, 768) for k in range(4)]
REDUCE_CHUNKS = [(0, 784), (784, 768), (1552, 768), (2320, 768)]
SHARED_ROWS = 8


def enter(d, s):
    barrier = pltpu.get_barrier_semaphore()
    for k in range(1, DP):
        pl.semaphore_signal(
            barrier, inc=1, device_id=(lax.rem(d + k, DP), s), device_id_type=MESH
        )
    for k in range(1, SEQ):
        pl.semaphore_signal(
            barrier, inc=1, device_id=(d, lax.rem(s + k, SEQ)), device_id_type=MESH
        )
    pl.semaphore_wait(barrier, DP - 1 + SEQ - 1)


def remote(src, dst, send_sem, recv_sem, device):
    return pltpu.make_async_remote_copy(
        src_ref=src,
        dst_ref=dst,
        send_sem=send_sem,
        recv_sem=recv_sem,
        device_id=device,
        device_id_type=MESH,
    )


def gather_kernel(
    mine, shared, full, shared_all, tails, row, send, recv_z, recv_x, s_send, s_recv, d_send, d_recv
):
    d, s = lax.axis_index("dp"), lax.axis_index("seq")
    z, x = d // 2, lax.rem(d, 2)
    parts = len(GATHER_CHUNKS) + 1
    full[pl.ds(pl.multiple_of(d * BLOCK, BLOCK), BLOCK), :] = mine[:BLOCK, :]
    tails[d] = mine[BLOCK:, :]
    row[s] = shared[...]
    enter(d, s)

    def piece(zp, xp, c):
        if c == parts - 1:
            return tails.at[2 * zp + xp]
        offset, size = GATHER_CHUNKS[c]
        return full.at[pl.ds(pl.multiple_of((2 * zp + xp) * BLOCK + offset, 256), size)]

    def up(zp, c):
        ref = piece(zp, x, c)
        return remote(ref, ref, send.at[0, zp, c], recv_z.at[zp, c], (2 * (z + 1) + x, s))

    def down(zp, c):
        ref = piece(zp, x, c)
        return remote(ref, ref, send.at[1, zp, c], recv_z.at[zp, c], (2 * (z - 1) + x, s))

    def across(zp, c):
        ref = piece(zp, x, c)
        return remote(ref, ref, send.at[2, zp, c], recv_x.at[zp, c], (2 * z + 1 - x, s))

    def to_share(k):
        ref = row.at[s]
        return remote(ref, ref, s_send.at[k], s_recv.at[s], (d, lax.rem(s + k, SEQ)))

    def from_share(k):
        other = lax.rem(s + k, SEQ)
        ref = row.at[other]
        return remote(ref, ref, s_send.at[k], s_recv.at[other], (d, other))

    def to_group(k):
        return remote(
            row, shared_all.at[d], d_send.at[k], d_recv.at[d], (lax.rem(d + k, DP), s)
        )

    def from_group(k):
        other = lax.rem(d + k, DP)
        return remote(row, shared_all.at[other], d_send.at[k], d_recv.at[other], (other, s))

    for k in range(1, SEQ):
        to_share(k).start()
    for c in range(parts):
        pl.when(z < Z - 1)(lambda: up(z, c).start())
        pl.when(z > 0)(lambda: down(z, c).start())
        across(z, c).start()
    for k in range(1, SEQ):
        from_share(k).wait_recv()
    shared_all[d] = row[...]
    for k in range(1, DP):
        to_group(k).start()
    for k in range(1, Z):
        for c in range(parts):

            @pl.when(z >= k)
            def _():
                up(z - k, c).wait_recv()
                pl.when(z < Z - 1)(lambda: up(z - k, c).start())
                across(z - k, c).start()

            @pl.when(z + k < Z)
            def _():
                down(z + k, c).wait_recv()
                pl.when(z > 0)(lambda: down(z + k, c).start())
                across(z + k, c).start()

    for zp in range(Z):
        for c in range(parts):
            ref = piece(zp, 1 - x, c)
            remote(
                ref, ref, send.at[2, zp, c], recv_x.at[zp, c], (2 * z + 1 - x, s)
            ).wait_recv()
            across(zp, c).wait_send()
            pl.when((z >= zp) & (z < Z - 1))(lambda: up(zp, c).wait_send())
            pl.when((z <= zp) & (z > 0))(lambda: down(zp, c).wait_send())
    for k in range(1, SEQ):
        to_share(k).wait_send()
    for k in range(1, DP):
        to_group(k).wait_send()
        from_group(k).wait_recv()
    for k in range(1, DP):
        head = full[k * BLOCK : k * BLOCK + EDGE, :].astype(jnp.float32)
        tail = tails[k - 1].astype(jnp.float32)
        full[k * BLOCK : k * BLOCK + EDGE, :] = (head + tail).astype(jnp.bfloat16)
    full[DP * BLOCK :, :] = tails[DP - 1]


def gather_parts(split_params, shared_params, dp_count, seq_count):
    rows = split_params.shape[1] // LANES
    d = lax.axis_index("dp")
    mine = lax.dynamic_update_slice(
        jnp.zeros((SPAN, LANES), jnp.bfloat16),
        split_params.reshape(rows, LANES).astype(jnp.bfloat16),
        (d, 0),
    )
    count = shared_params.shape[0]
    padded = jnp.pad(shared_params, (0, SHARED_ROWS * LANES - count))
    vmem = pl.BlockSpec(memory_space=pltpu.VMEM)
    parts = len(GATHER_CHUNKS) + 1
    dma = pltpu.SemaphoreType.DMA
    full, shared_all = pl.pallas_call(
        gather_kernel,
        out_shape=(
            jax.ShapeDtypeStruct((DP * BLOCK + EDGE, LANES), jnp.bfloat16),
            jax.ShapeDtypeStruct((DP, SEQ, SHARED_ROWS, LANES), jnp.float32),
        ),
        in_specs=[vmem, vmem],
        out_specs=(vmem, vmem),
        scratch_shapes=[
            pltpu.VMEM((DP, EDGE, LANES), jnp.bfloat16),
            pltpu.VMEM((SEQ, SHARED_ROWS, LANES), jnp.float32),
            dma((3, Z, parts)),
            dma((Z, parts)),
            dma((Z, parts)),
            dma((SEQ,)),
            dma((SEQ,)),
            dma((DP,)),
            dma((DP,)),
        ],
        compiler_params=pltpu.CompilerParams(
            collective_id=0, has_side_effects=True, vmem_limit_bytes=24 * 2**20
        ),
        cost_estimate=pl.CostEstimate(flops=0, bytes_accessed=200 * 2**20, transcendentals=0),
        name="gather_params",
    )(mine, padded.reshape(SHARED_ROWS, LANES))
    shared_full = shared_all.reshape(DP * SEQ, SHARED_ROWS * LANES)[:, :count].reshape(-1)
    return full, shared_full


def reduce_kernel(
    flat,
    shared,
    out,
    shared_out,
    x_in,
    up_in,
    down_in,
    stage,
    share_in,
    share_sum,
    group_in,
    x_send,
    x_recv,
    z_send,
    up_recv,
    down_recv,
    s_send,
    s_recv,
    d_send,
    d_recv,
):
    d, s = lax.axis_index("dp"), lax.axis_index("seq")
    z, x = d // 2, lax.rem(d, 2)
    f32 = jnp.float32
    enter(d, s)

    def across(zp, c):
        offset, size = REDUCE_CHUNKS[c]
        start = pl.multiple_of((2 * zp + 1 - x) * BLOCK + offset, EDGE)
        return remote(
            flat.at[pl.ds(start, size)],
            x_in.at[zp, pl.ds(offset, size)],
            x_send.at[zp, c],
            x_recv.at[zp, c],
            (2 * z + 1 - x, s),
        )

    def along(zp, c, step, into, recv):
        offset, size = REDUCE_CHUNKS[c]
        return remote(
            stage.at[zp, pl.ds(offset, size)],
            into.at[zp, pl.ds(offset, size)],
            z_send.at[zp, c],
            recv.at[zp, c],
            (2 * (z + step) + x, s),
        )

    def up(zp, c):
        return along(zp, c, 1, up_in, up_recv)

    def down(zp, c):
        return along(zp, c, -1, down_in, down_recv)

    def add(zp, c, others, store):
        offset, size = REDUCE_CHUNKS[c]
        tile = 112 if size % 128 else 128

        def body(k, carry):
            at = pl.multiple_of(offset + k * tile, EDGE)
            own = pl.multiple_of((2 * zp + x) * BLOCK + offset + k * tile, EDGE)
            total = flat[pl.ds(own, tile), :].astype(f32)
            for ref in (x_in, *others):
                total = total + ref[zp, pl.ds(at, tile), :].astype(f32)
            store(at, tile, total)
            return carry

        lax.fori_loop(0, size // tile, body, 0)

    def hop(zp, c, others, copy):
        def store(at, tile, total):
            stage[zp, pl.ds(at, tile), :] = total.astype(jnp.bfloat16)

        add(zp, c, others, store)
        copy.start()

    def to_share(k):
        other = lax.rem(s + k, SEQ)
        return remote(
            shared.at[other], share_in.at[s], s_send.at[k], s_recv.at[s], (d, other)
        )

    def from_share(k):
        other = lax.rem(s + k, SEQ)
        return remote(
            shared.at[s], share_in.at[other], s_send.at[k], s_recv.at[other], (d, other)
        )

    def to_group(k):
        other = lax.rem(d + k, DP)
        return remote(
            share_sum.at[other], group_in.at[d], d_send.at[k], d_recv.at[d], (other, s)
        )

    def from_group(k):
        other = lax.rem(d + k, DP)
        return remote(
            share_sum.at[d], group_in.at[other], d_send.at[k], d_recv.at[other], (other, s)
        )

    chunks = range(len(REDUCE_CHUNKS))
    items = [(zp, c) for c in chunks for zp in (Z - 1, 0)]
    items += [(zp, c) for c in chunks for zp in (2, 1)]
    ahead = 6
    for k in range(1, SEQ):
        to_share(k).start()
    for zp, c in items[:ahead]:
        across(zp, c).start()
    share_in[s] = shared[s]
    for k in range(1, SEQ):
        from_share(k).wait_recv()
    share_sum[...] = share_in[0] + share_in[1] + share_in[2] + share_in[3]
    for k in range(1, DP):
        to_group(k).start()
    group_in[d] = share_sum[d]

    for t, (zp, c) in enumerate(items):
        if t + ahead < len(items):
            across(*items[t + ahead]).start()

        @pl.when(z != zp)
        def _():
            across(zp, c).wait_recv()

        if zp > 0:

            @pl.when(z == 0)
            def _():
                hop(zp, c, (), up(zp, c))

        if zp > 1:

            @pl.when((z > 0) & (z < zp))
            def _():
                up(zp, c).wait_recv()
                hop(zp, c, (up_in,), up(zp, c))

        if zp < Z - 1:

            @pl.when(z == Z - 1)
            def _():
                hop(zp, c, (), down(zp, c))

        if zp < Z - 2:

            @pl.when((z < Z - 1) & (z > zp))
            def _():
                down(zp, c).wait_recv()
                hop(zp, c, (down_in,), down(zp, c))

    def keep(at, tile, total):
        out[pl.ds(at, tile), :] = total

    for c in chunks:
        across(z, c).wait_recv()

        @pl.when(z == 0)
        def _():
            down(z, c).wait_recv()
            add(z, c, (down_in,), keep)

        @pl.when(z == Z - 1)
        def _():
            up(z, c).wait_recv()
            add(z, c, (up_in,), keep)

        @pl.when((z > 0) & (z < Z - 1))
        def _():
            up(z, c).wait_recv()
            down(z, c).wait_recv()
            add(z, c, (up_in, down_in), keep)

    for zp, c in items:
        across(zp, c).wait_send()
        pl.when(z < zp)(lambda: up(zp, c).wait_send())
        pl.when(z > zp)(lambda: down(zp, c).wait_send())
    for k in range(1, SEQ):
        to_share(k).wait_send()
    for k in range(1, DP):
        to_group(k).wait_send()
        from_group(k).wait_recv()
    total = group_in[0]
    for k in range(1, DP):
        total = total + group_in[k]
    shared_out[...] = total


def reduce_parts(flat, shared_flat, dp_count, seq_count):
    d = lax.axis_index("dp")
    rows = flat.shape[0] // dp_count
    count = shared_flat.shape[0] // (DP * SEQ)
    flat = jnp.pad(flat, ((0, DP * BLOCK + EDGE - flat.shape[0]), (0, 0)))
    shared = jnp.pad(
        shared_flat.reshape(DP, SEQ, count), ((0, 0), (0, 0), (0, SHARED_ROWS * LANES - count))
    )
    shared = shared.transpose(1, 0, 2).reshape(SEQ, DP, SHARED_ROWS, LANES)
    vmem = pl.BlockSpec(memory_space=pltpu.VMEM)
    dma = pltpu.SemaphoreType.DMA
    held = pltpu.VMEM((Z, SPAN, LANES), jnp.bfloat16)
    sems = dma((Z, len(REDUCE_CHUNKS)))
    out, shared_out = pl.pallas_call(
        reduce_kernel,
        out_shape=(
            jax.ShapeDtypeStruct((SPAN, LANES), jnp.float32),
            jax.ShapeDtypeStruct((SHARED_ROWS, LANES), jnp.float32),
        ),
        in_specs=[vmem, vmem],
        out_specs=(vmem, vmem),
        scratch_shapes=[
            held,
            held,
            held,
            held,
            pltpu.VMEM((SEQ, DP, SHARED_ROWS, LANES), jnp.float32),
            pltpu.VMEM((DP, SHARED_ROWS, LANES), jnp.float32),
            pltpu.VMEM((DP, SHARED_ROWS, LANES), jnp.float32),
            sems,
            sems,
            sems,
            sems,
            sems,
            dma((SEQ,)),
            dma((SEQ,)),
            dma((DP,)),
            dma((DP,)),
        ],
        compiler_params=pltpu.CompilerParams(
            collective_id=1, has_side_effects=True, vmem_limit_bytes=40 * 2**20
        ),
        cost_estimate=pl.CostEstimate(flops=0, bytes_accessed=250 * 2**20, transcendentals=0),
        name="reduce_grads",
    )(flat, shared)
    grads = lax.dynamic_slice(out, (d, 0), (rows, LANES)).reshape(1, rows * LANES)
    return grads, shared_out.reshape(-1)[:count]


def attend(queries, keys_rot, values, segment_row):
    length = queries.shape[1]
    ids = jnp.arange(length, dtype=jnp.int32)
    allowed = (segment_row[:, None] == segment_row[None, :]) & (ids[:, None] >= ids[None, :])
    scores = jnp.einsum("hid,hjd->hij", queries, keys_rot, preferred_element_type=jnp.float32)
    scores = jnp.where(allowed[None], scores * HEAD_DIM ** (-0.5), masked_score)
    row_max = jnp.max(scores, -1, keepdims=True)
    log_total = row_max + jnp.log(jnp.sum(jnp.exp(scores - row_max), -1, keepdims=True))
    prob = jnp.exp(scores - log_total)
    prob_low = prob.astype(jnp.bfloat16)
    attended = jnp.einsum("hij,hjd->hid", prob_low, values, preferred_element_type=jnp.float32)
    return attended.astype(jnp.bfloat16), prob, prob_low


def attend_back(queries, keys_rot, values, attended, prob, prob_low, grad_att):
    delta = jnp.sum(grad_att.astype(jnp.float32) * attended.astype(jnp.float32), -1, keepdims=True)
    grad_values = jnp.einsum("hij,hid->hjd", prob_low, grad_att, preferred_element_type=jnp.float32)
    grad_prob = jnp.einsum("hid,hjd->hij", grad_att, values, preferred_element_type=jnp.float32)
    grad_scores = (prob * (grad_prob - delta) * HEAD_DIM ** (-0.5)).astype(jnp.bfloat16)
    grad_query = jnp.einsum(
        "hij,hjd->hid", grad_scores, keys_rot, preferred_element_type=jnp.float32
    )
    grad_keys = jnp.einsum("hij,hid->hjd", grad_scores, queries, preferred_element_type=jnp.float32)
    return grad_query, grad_keys, grad_values


def local_grouped(
    hidden_in,
    cotangent,
    segments,
    shared_params,
    split_params,
    shared_m1,
    split_m1,
    shared_m2,
    split_m2,
):
    dp_count = lax.axis_size("dp")
    seq_count = lax.axis_size("seq")
    share = lax.axis_index("seq")
    heads_here = HEADS // seq_count
    ql = 3 * MODEL_WIDTH // seq_count
    dl = MODEL_WIDTH // seq_count
    fl = FF // seq_count
    f32, bf16 = jnp.float32, jnp.bfloat16
    tokens_here = hidden_in.shape[0]
    both = lax.all_gather(
        jnp.concatenate([hidden_in, cotangent], 1), "seq", axis=0, tiled=True
    )
    group_hidden, group_cot = both[:, :MODEL_WIDTH], both[:, MODEL_WIDTH:]
    full, shared_full = gather_parts(split_params, shared_params, dp_count, seq_count)
    b_qkv, b_dense, b_proj, gain_one, shift_one, gain_two, shift_two = unpack_shared(shared_full)
    extents = share_layout(seq_count)
    offsets = [sum(extents[:k]) for k in range(6)]
    w_qkv, w_dense, w_fc, b_fc, w_proj = [
        full[offsets[k] : offsets[k + 1]].reshape(shape)
        for k, shape in enumerate(
            [(MODEL_WIDTH, ql), (dl, MODEL_WIDTH), (MODEL_WIDTH, fl), (fl,), (fl, MODEL_WIDTH)]
        )
    ]
    b_fc = b_fc.astype(f32)
    b_qkv_mine = lax.dynamic_slice(b_qkv, (share * ql,), (ql,))

    resid = group_hidden.astype(f32)
    first_norm, normed, root = layer_norm(resid, gain_one, shift_one)
    first_low = first_norm.astype(bf16)
    second_low = (normed * gain_two + shift_two).astype(bf16)
    length = resid.shape[0]

    qkv = (jnp.dot(first_low, w_qkv, preferred_element_type=f32) + b_qkv_mine).astype(bf16)
    qkv = qkv.reshape(length, heads_here, 3, HEAD_DIM).transpose(2, 1, 0, 3)
    segment_row = segments[0]
    cosines, sines = rotary_tables(segment_row)
    cosines, sines = cosines[:, 0], sines[:, 0]
    queries = rotate(qkv[0].astype(f32), cosines, sines, 1.0).astype(bf16)
    keys_rot = rotate(qkv[1].astype(f32), cosines, sines, 1.0).astype(bf16)
    values = qkv[2]
    attended, prob, prob_low = attend(queries, keys_rot, values, segment_row)
    att_flat = attended.transpose(1, 0, 2).reshape(length, dl)

    hidden_pre = jnp.dot(second_low, w_fc, preferred_element_type=f32) + b_fc
    activated = jax.nn.gelu(hidden_pre, approximate=False).astype(bf16)
    branch = jnp.dot(att_flat, w_dense, preferred_element_type=f32) + jnp.dot(
        activated, w_proj, preferred_element_type=f32
    )
    total = lax.psum_scatter(branch, "seq", scatter_dimension=0, tiled=True)
    output = (hidden_in.astype(f32) + total + b_dense + b_proj).astype(bf16)

    grad_outf = cotangent.astype(f32)
    grad_b_out = jnp.sum(grad_outf, 0)
    grad_w_proj = jnp.dot(activated.T, group_cot, preferred_element_type=f32)
    grad_hidden = jnp.dot(group_cot, w_proj.T, preferred_element_type=f32) * gelu_slope(hidden_pre)
    grad_b_fc = jnp.sum(grad_hidden, 0)
    grad_hidden_low = grad_hidden.astype(bf16)
    grad_w_fc = jnp.dot(second_low.T, grad_hidden_low, preferred_element_type=f32)
    grad_second = jnp.dot(grad_hidden_low, w_fc.T, preferred_element_type=f32)
    grad_w_dense = jnp.dot(att_flat.T, group_cot, preferred_element_type=f32)
    grad_att = (
        jnp.dot(group_cot, w_dense.T, preferred_element_type=f32)
        .astype(bf16)
        .reshape(length, heads_here, HEAD_DIM)
        .transpose(1, 0, 2)
    )
    grad_query, grad_keys, grad_values = attend_back(
        queries, keys_rot, values, attended, prob, prob_low, grad_att
    )
    grad_query = rotate(grad_query, cosines, sines, -1.0)
    grad_keys = rotate(grad_keys, cosines, sines, -1.0)
    grad_qkv = (
        jnp.stack([grad_query, grad_keys, grad_values])
        .astype(bf16)
        .transpose(2, 1, 0, 3)
        .reshape(length, ql)
    )
    grad_b_qkv = jnp.sum(grad_qkv.astype(f32), 0)
    grad_w_qkv = jnp.dot(first_low.T, grad_qkv, preferred_element_type=f32)
    grad_first = jnp.dot(grad_qkv, w_qkv.T, preferred_element_type=f32)

    scaled = lax.psum_scatter(
        gain_one * grad_first + gain_two * grad_second, "seq", scatter_dimension=0, tiled=True
    )
    normed_mine = lax.dynamic_slice(normed, (share * tokens_here, 0), (tokens_here, MODEL_WIDTH))
    root_mine = lax.dynamic_slice(root, (share * tokens_here, 0), (tokens_here, 1))
    input_grad = grad_outf + norm_back(scaled, 1.0, normed_mine, root_mine)

    shared_flat = jnp.concatenate(
        [
            lax.dynamic_update_slice(
                jnp.zeros((3 * MODEL_WIDTH,), f32), grad_b_qkv, (share * ql,)
            ),
            grad_b_out,
            grad_b_out,
            jnp.sum(grad_first * normed, 0),
            jnp.sum(grad_first, 0),
            jnp.sum(grad_second * normed, 0),
            jnp.sum(grad_second, 0),
        ]
    )
    flat = jnp.concatenate(
        [
            part.astype(bf16).reshape(-1, LANES)
            for part in (grad_w_qkv, grad_w_dense, grad_w_fc, grad_b_fc, grad_w_proj)
        ]
    )
    split_grads, shared_grads = reduce_parts(flat, shared_flat, dp_count, seq_count)
    shared_new, shared_m1_new, shared_m2_new = adamw(
        shared_params, shared_m1, shared_m2, shared_grads
    )
    split_new, split_m1_new, split_m2_new = adamw(split_params, split_m1, split_m2, split_grads)
    return (
        output,
        input_grad,
        shared_grads,
        split_grads,
        shared_new,
        split_new,
        shared_m1_new,
        split_m1_new,
        shared_m2_new,
        split_m2_new,
    )


def solution(mesh):
    in_specs = (
        P(("dp", "seq"), None),
        P(("dp", "seq"), None),
        P("dp", None),
        P(("dp", "seq")),
        P("seq", "dp"),
        P(("dp", "seq")),
        P("seq", "dp"),
        P(("dp", "seq")),
        P("seq", "dp"),
    )
    out_specs = (
        P(("dp", "seq"), None),
        P(("dp", "seq"), None),
        P(("dp", "seq")),
        P("seq", "dp"),
        P(("dp", "seq")),
        P("seq", "dp"),
        P(("dp", "seq")),
        P("seq", "dp"),
        P(("dp", "seq")),
        P("seq", "dp"),
    )
    dp_count, seq_count = mesh.shape["dp"], mesh.shape["seq"]
    local = local_grouped if (dp_count, seq_count) == (DP, SEQ) else local_general
    return jax.shard_map(local, mesh=mesh, in_specs=in_specs, out_specs=out_specs, check_vma=False)
```

```python
import math

import jax
import jax.numpy as jnp
from jax import lax
from jax.experimental import pallas as pl
from jax.experimental.pallas import tpu as pltpu
from jax.sharding import PartitionSpec as P

MODEL_WIDTH = 1024
HEADS = 16
HEAD_DIM = 64
FF = 4096
ROT = 16
STEP = 3


norm_eps = 1e-05
beta_first = 0.9
beta_second = 0.95
adam_eps = 1e-08
learn_rate = 0.1
weight_decay = 0.01
rotary_base = 10000.0
masked_score = -1e30


def unpack_shared(flat_vec):
    extents = [
        (3 * MODEL_WIDTH,),
        (MODEL_WIDTH,),
        (MODEL_WIDTH,),
        (MODEL_WIDTH,),
        (MODEL_WIDTH,),
        (MODEL_WIDTH,),
        (MODEL_WIDTH,),
    ]
    pieces = []
    offset = 0
    for extent in extents:
        number = math.prod(extent)
        pieces.append(flat_vec[offset : offset + number])
        offset = offset + number
    return pieces


def unpack_split(matrix, seq_count):
    rows = matrix.shape[0]
    qkv_part = 3 * MODEL_WIDTH // seq_count
    dense_output_slice = MODEL_WIDTH // seq_count
    hidden_units_slice = FF // seq_count
    zero_end = MODEL_WIDTH * qkv_part
    first_end = zero_end + dense_output_slice * MODEL_WIDTH
    second_end = first_end + MODEL_WIDTH * hidden_units_slice
    third_end = second_end + hidden_units_slice
    w_qkv = (
        matrix[:, :zero_end]
        .reshape(rows, MODEL_WIDTH, qkv_part)
        .transpose(1, 0, 2)
        .reshape(MODEL_WIDTH, rows * qkv_part)
    )
    dense_weight = matrix[:, zero_end:first_end].reshape(rows * dense_output_slice, MODEL_WIDTH)
    expand_weight = (
        matrix[:, first_end:second_end]
        .reshape(rows, MODEL_WIDTH, hidden_units_slice)
        .transpose(1, 0, 2)
        .reshape(MODEL_WIDTH, rows * hidden_units_slice)
    )
    b_fc = matrix[:, second_end:third_end].reshape(rows * hidden_units_slice)
    contract_weight = matrix[:, third_end:].reshape(rows * hidden_units_slice, MODEL_WIDTH)
    return (w_qkv, dense_weight, expand_weight, b_fc, contract_weight)


def pack_split(w_qkv, dense_weight, expand_weight, b_fc, contract_weight, seq_count):
    qkv_part = 3 * MODEL_WIDTH // seq_count
    dense_output_slice = MODEL_WIDTH // seq_count
    hidden_units_slice = FF // seq_count
    rows = dense_weight.shape[0] // dense_output_slice
    return jnp.concatenate(
        [
            w_qkv.reshape(MODEL_WIDTH, rows, qkv_part)
            .transpose(1, 0, 2)
            .reshape(rows, MODEL_WIDTH * qkv_part),
            dense_weight.reshape(rows, dense_output_slice * MODEL_WIDTH),
            expand_weight.reshape(MODEL_WIDTH, rows, hidden_units_slice)
            .transpose(1, 0, 2)
            .reshape(rows, MODEL_WIDTH * hidden_units_slice),
            b_fc.reshape(rows, hidden_units_slice),
            contract_weight.reshape(rows, hidden_units_slice * MODEL_WIDTH),
        ],
        1,
    )


def adamw(param_vals, first_m, second_m, grad_vals):
    first_new = beta_first * first_m + (1.0 - beta_first) * grad_vals
    second_new = beta_second * second_m + (1.0 - beta_second) * grad_vals * grad_vals
    first_hat = first_new / (1.0 - beta_first**STEP)
    second_hat = second_new / (1.0 - beta_second**STEP)
    param_new = param_vals - learn_rate * (
        first_hat / (jnp.sqrt(second_hat) + adam_eps) + weight_decay * param_vals
    )
    return (param_new, first_new, second_new)


def layer_norm(resid, gain_vec, shift_vec):
    average = jnp.mean(resid, -1, keepdims=True)
    centered = resid - average
    variance = jnp.mean(centered * centered, -1, keepdims=True)
    recip_root = lax.rsqrt(variance + norm_eps)
    normed = centered * recip_root
    return (normed * gain_vec + shift_vec, normed, recip_root)


def norm_back(grad_norm, gain_vec, normed, recip_root):
    scaled = grad_norm * gain_vec
    return recip_root * (
        scaled
        - jnp.mean(scaled, -1, keepdims=True)
        - normed * jnp.mean(scaled * normed, -1, keepdims=True)
    )


def gelu_slope(inputs):
    normal_cdf = 0.5 * (1.0 + jax.scipy.special.erf(inputs * 0.7071067811865476))
    return normal_cdf + inputs * jnp.exp(-0.5 * inputs * inputs) * 0.3989422804014327


def rotary_tables(segment_row):
    indices = jnp.arange(segment_row.shape[0], dtype=jnp.int32)
    change = jnp.concatenate([jnp.ones((1,), dtype=jnp.bool_), segment_row[1:] != segment_row[:-1]])
    starts = lax.cummax(jnp.where(change, indices, jnp.zeros_like(indices)), axis=0)
    positions = (indices - starts).astype(jnp.float32)
    frequency = rotary_base ** (-jnp.arange(0, ROT, 2, dtype=jnp.float32) / ROT)
    angles = positions[:, None] * frequency[None, :]
    return (jnp.cos(angles)[:, None, :], jnp.sin(angles)[:, None, :])


def rotate(field, cosines, sines, direction):
    half_rot = ROT // 2
    first_half = field[..., :half_rot]
    second = field[..., half_rot:ROT]
    return jnp.concatenate(
        [
            first_half * cosines - direction * second * sines,
            second * cosines + direction * first_half * sines,
            field[..., ROT:],
        ],
        -1,
    )


def score_block(query_block, keys_rot, seg_block, row_ids, segment_row, col_ids):
    scale = HEAD_DIM ** (-0.5)
    scores = (
        jnp.einsum("ihd,jhd->hij", query_block, keys_rot, preferred_element_type=jnp.float32)
        * scale
    )
    allowed = (seg_block[:, None] == segment_row[None, :]) & (row_ids[:, None] >= col_ids[None, :])
    return jnp.where(allowed[None], scores, masked_score)


def attention_forward(queries, keys_rot, values, segment_row):
    segment_length, heads_here, head_size = queries.shape
    block_rows = min(512, segment_length)
    block_count = segment_length // block_rows
    col_ids = jnp.arange(segment_length, dtype=jnp.int32)

    def one_block(packed):
        query_block, seg_block, row_ids = packed
        scores = score_block(query_block, keys_rot, seg_block, row_ids, segment_row, col_ids)
        row_max = jnp.max(scores, -1, keepdims=True)
        log_total = row_max[..., 0] + jnp.log(jnp.sum(jnp.exp(scores - row_max), -1))
        probability = jnp.exp(scores - log_total[..., None]).astype(jnp.bfloat16)
        attended = jnp.einsum(
            "hij,jhd->ihd", probability, values, preferred_element_type=jnp.float32
        ).astype(jnp.bfloat16)
        return (attended, log_total)

    attended, log_totals = lax.map(
        one_block,
        (
            queries.reshape(block_count, block_rows, heads_here, head_size),
            segment_row.reshape(block_count, block_rows),
            col_ids.reshape(block_count, block_rows),
        ),
    )
    return (attended.reshape(segment_length, heads_here, head_size), log_totals)


def attention_backward(queries, keys_rot, values, attended, log_totals, grad_att, segment_row):
    segment_length, heads_here, head_size = queries.shape
    block_rows = min(512, segment_length)
    block_count = segment_length // block_rows
    col_ids = jnp.arange(segment_length, dtype=jnp.int32)
    scale = HEAD_DIM ** (-0.5)

    def one_block(running, packed):
        grad_keys, grad_values = running
        query_block, out_block, grad_block, log_total, seg_block, row_ids = packed
        scores = score_block(query_block, keys_rot, seg_block, row_ids, segment_row, col_ids)
        probability = jnp.exp(scores - log_total[..., None])
        prob_low = probability.astype(jnp.bfloat16)
        delta = jnp.sum(grad_block.astype(jnp.float32) * out_block.astype(jnp.float32), -1).T
        grad_values = grad_values + jnp.einsum(
            "hij,ihd->jhd", prob_low, grad_block, preferred_element_type=jnp.float32
        )
        grad_prob = jnp.einsum(
            "ihd,jhd->hij", grad_block, values, preferred_element_type=jnp.float32
        )
        grad_scores = (probability * (grad_prob - delta[..., None]) * scale).astype(jnp.bfloat16)
        grad_query = jnp.einsum(
            "hij,jhd->ihd", grad_scores, keys_rot, preferred_element_type=jnp.float32
        )
        grad_keys = grad_keys + jnp.einsum(
            "hij,ihd->jhd", grad_scores, query_block, preferred_element_type=jnp.float32
        )
        return ((grad_keys, grad_values), grad_query)

    zero_field = jnp.zeros((segment_length, heads_here, head_size), jnp.float32)
    shaped = (
        queries.reshape(block_count, block_rows, heads_here, head_size),
        attended.reshape(block_count, block_rows, heads_here, head_size),
        grad_att.reshape(block_count, block_rows, heads_here, head_size),
        log_totals,
        segment_row.reshape(block_count, block_rows),
        col_ids.reshape(block_count, block_rows),
    )
    (grad_keys, grad_values), grad_query = lax.scan(one_block, (zero_field, zero_field), shaped)
    return (grad_query.reshape(segment_length, heads_here, head_size), grad_keys, grad_values)


def local_general(
    hidden_in,
    cotangent,
    segments,
    shared_params,
    split_params,
    shared_m1,
    split_m1,
    shared_m2,
    split_m2,
):
    tokens_here = hidden_in.shape[0]
    seq_count = lax.axis_size("seq")
    heads_here = HEADS // seq_count
    qkv_cols = 3 * MODEL_WIDTH // seq_count
    shared_full = lax.all_gather(shared_params, ("dp", "seq"), axis=0, tiled=True)
    b_qkv, b_dense, b_proj, gain_one, shift_one, gain_two, shift_two = unpack_shared(shared_full)
    split_mine = lax.all_gather(split_params.astype(jnp.bfloat16), "dp", axis=1, tiled=True)
    w_qkv_share, dense_weight, expand_weight, b_fc, contract_weight = unpack_split(
        split_mine, seq_count
    )
    b_fc = b_fc.astype(jnp.float32)
    column_rows = lax.all_gather(split_mine[:, : MODEL_WIDTH * qkv_cols], "seq", axis=0, tiled=True)
    w_qkv = (
        column_rows.reshape(seq_count, MODEL_WIDTH, qkv_cols)
        .transpose(1, 0, 2)
        .reshape(MODEL_WIDTH, 3 * MODEL_WIDTH)
    )
    resid = hidden_in.astype(jnp.float32)
    first_norm, normed_one, root_one = layer_norm(resid, gain_one, shift_one)
    second_norm, normed_two, root_two = layer_norm(resid, gain_two, shift_two)
    first_low = first_norm.astype(jnp.bfloat16)
    second_low = second_norm.astype(jnp.bfloat16)
    group_first, group_norm, group_cot = (
        lax.all_gather(first_low, "seq", axis=0, tiled=True),
        lax.all_gather(second_low, "seq", axis=0, tiled=True),
        lax.all_gather(cotangent, "seq", axis=0, tiled=True),
    )
    group_length = group_first.shape[0]
    qkv = (
        (jnp.dot(first_low, w_qkv, preferred_element_type=jnp.float32) + b_qkv)
        .astype(jnp.bfloat16)
        .reshape(tokens_here, HEADS, 3 * HEAD_DIM)
    )
    grouped = lax.all_to_all(qkv, "seq", split_axis=1, concat_axis=0, tiled=True)
    segment_row = segments[0]
    cosines, sines = rotary_tables(segment_row)
    queries = rotate(grouped[..., :HEAD_DIM].astype(jnp.float32), cosines, sines, 1.0).astype(
        jnp.bfloat16
    )
    keys_rot = rotate(
        grouped[..., HEAD_DIM : 2 * HEAD_DIM].astype(jnp.float32), cosines, sines, 1.0
    ).astype(jnp.bfloat16)
    values = grouped[..., 2 * HEAD_DIM :]
    attended, log_totals = attention_forward(queries, keys_rot, values, segment_row)
    grad_outf = cotangent.astype(jnp.float32)
    grad_b_proj = jnp.sum(grad_outf, 0)
    grad_b_dense = jnp.sum(grad_outf, 0)
    att_flat = attended.reshape(group_length, heads_here * HEAD_DIM)
    hidden_pre = jnp.dot(group_norm, expand_weight, preferred_element_type=jnp.float32) + b_fc
    hidden_activations = jax.nn.gelu(hidden_pre, approximate=False).astype(jnp.bfloat16)
    branch = jnp.dot(att_flat, dense_weight, preferred_element_type=jnp.float32) + jnp.dot(
        hidden_activations, contract_weight, preferred_element_type=jnp.float32
    )
    total = (
        resid + lax.psum_scatter(branch, "seq", scatter_dimension=0, tiled=True) + b_dense + b_proj
    )
    output = total.astype(jnp.bfloat16)
    grad_w_proj = jnp.dot(hidden_activations.T, group_cot, preferred_element_type=jnp.float32)
    grad_hidden = jnp.dot(
        group_cot, contract_weight.T, preferred_element_type=jnp.float32
    ) * gelu_slope(hidden_pre)
    grad_b_fc = jnp.sum(grad_hidden, 0)
    hidden_reduced_precision = grad_hidden.astype(jnp.bfloat16)
    grad_w_fc = jnp.dot(group_norm.T, hidden_reduced_precision, preferred_element_type=jnp.float32)
    grad_second = lax.psum_scatter(
        jnp.dot(hidden_reduced_precision, expand_weight.T, preferred_element_type=jnp.float32),
        "seq",
        scatter_dimension=0,
        tiled=True,
    )
    grad_w_dense = jnp.dot(att_flat.T, group_cot, preferred_element_type=jnp.float32)
    grad_att_heads = (
        jnp.dot(group_cot, dense_weight.T, preferred_element_type=jnp.float32)
        .astype(jnp.bfloat16)
        .reshape(group_length, heads_here, HEAD_DIM)
    )
    grad_query, grad_keys, grad_values = attention_backward(
        queries, keys_rot, values, attended, log_totals, grad_att_heads, segment_row
    )
    grad_query = rotate(grad_query, cosines, sines, -1.0)
    grad_keys = rotate(grad_keys, cosines, sines, -1.0)
    grad_grouped = jnp.concatenate([grad_query, grad_keys, grad_values], -1).astype(jnp.bfloat16)
    grad_w_qkv_share = jnp.dot(
        group_first.T,
        grad_grouped.reshape(group_length, qkv_cols),
        preferred_element_type=jnp.float32,
    )
    grad_qkv = lax.all_to_all(grad_grouped, "seq", split_axis=0, concat_axis=1, tiled=True).reshape(
        tokens_here, 3 * MODEL_WIDTH
    )
    grad_b_qkv = jnp.sum(grad_qkv.astype(jnp.float32), 0)
    grad_first = jnp.dot(grad_qkv, w_qkv.T, preferred_element_type=jnp.float32)
    grad_gain_one = jnp.sum(grad_first * normed_one, 0)
    grad_shift_one = jnp.sum(grad_first, 0)
    grad_gain_two = jnp.sum(grad_second * normed_two, 0)
    grad_shift_two = jnp.sum(grad_second, 0)
    input_grad = (
        grad_outf
        + norm_back(grad_first, gain_one, normed_one, root_one)
        + norm_back(grad_second, gain_two, normed_two, root_two)
    )
    shared_flat = jnp.concatenate(
        [
            grad_b_qkv,
            grad_b_dense,
            grad_b_proj,
            grad_gain_one,
            grad_shift_one,
            grad_gain_two,
            grad_shift_two,
        ]
    )
    shared_grads = lax.psum_scatter(shared_flat, ("dp", "seq"), scatter_dimension=0, tiled=True)
    split_local = pack_split(
        grad_w_qkv_share, grad_w_dense, grad_w_fc, grad_b_fc, grad_w_proj, seq_count
    )
    split_grads = lax.psum_scatter(split_local, "dp", scatter_dimension=1, tiled=True)
    shared_new, shared_m1_new, shared_m2_new = adamw(
        shared_params, shared_m1, shared_m2, shared_grads
    )
    split_new, split_m1_new, split_m2_new = adamw(split_params, split_m1, split_m2, split_grads)
    return (
        output,
        input_grad,
        shared_grads,
        split_grads,
        shared_new,
        split_new,
        shared_m1_new,
        split_m1_new,
        shared_m2_new,
        split_m2_new,
    )


LANES = 128


def share_layout(seq_count):
    ql = 3 * MODEL_WIDTH // seq_count
    dl = MODEL_WIDTH // seq_count
    fl = FF // seq_count
    return [
        MODEL_WIDTH * ql // LANES,
        dl * MODEL_WIDTH // LANES,
        MODEL_WIDTH * fl // LANES,
        fl // LANES,
        fl * MODEL_WIDTH // LANES,
    ]


Z = 4
DP = 2 * Z
SEQ = 4
BLOCK = 3072
EDGE = 16
SPAN = BLOCK + EDGE
MESH = pl.DeviceIdType.MESH
GATHER_CHUNKS = [(k * 768, 768) for k in range(4)]
REDUCE_CHUNKS = [(0, 784), (784, 768), (1552, 768), (2320, 768)]
SHARED_ROWS = 8
PLACE_ROWS = 256
STEP_ROWS = 448
SUM_ROWS = 7 * STEP_ROWS + EDGE


def enter(d, s):
    barrier = pltpu.get_barrier_semaphore()
    for k in range(1, DP):
        pl.semaphore_signal(
            barrier, inc=1, device_id=(lax.rem(d + k, DP), s), device_id_type=MESH
        )
    for k in range(1, SEQ):
        pl.semaphore_signal(
            barrier, inc=1, device_id=(d, lax.rem(s + k, SEQ)), device_id_type=MESH
        )
    pl.semaphore_wait(barrier, DP - 1 + SEQ - 1)


def remote(src, dst, send_sem, recv_sem, device):
    return pltpu.make_async_remote_copy(
        src_ref=src,
        dst_ref=dst,
        send_sem=send_sem,
        recv_sem=recv_sem,
        device_id=device,
        device_id_type=MESH,
    )


def gather_kernel(
    source, shared, full, shared_all, load, mine, placed, tails, row, send, recv_z, recv_x, s_send, s_recv, d_send, d_recv
):
    d, s = lax.axis_index("dp"), lax.axis_index("seq")
    z, x = d // 2, lax.rem(d, 2)
    parts = len(GATHER_CHUNKS) + 1
    fetch = pltpu.make_async_copy(source.at[:, 0, :], mine, load)
    fetch.start()
    fetch.wait()
    rows = mine.shape[0]
    edge = jnp.zeros((EDGE, LANES), jnp.float32)
    placed[:EDGE, :] = edge
    placed[BLOCK:, :] = edge
    for offset in range(0, rows, PLACE_ROWS):
        size = min(PLACE_ROWS, rows - offset)
        placed[pl.ds(d + offset, size), :] = mine[offset : offset + size, :]
    for offset in range(0, BLOCK, PLACE_ROWS):
        at = pl.multiple_of(d * BLOCK + offset, PLACE_ROWS)
        full[pl.ds(at, PLACE_ROWS), :] = placed[offset : offset + PLACE_ROWS, :].astype(full.dtype)
    tails[d] = placed[BLOCK:, :].astype(full.dtype)
    row[s] = shared[...]
    enter(d, s)

    def piece(zp, xp, c):
        if c == parts - 1:
            return tails.at[2 * zp + xp]
        offset, size = GATHER_CHUNKS[c]
        return full.at[pl.ds(pl.multiple_of((2 * zp + xp) * BLOCK + offset, 256), size)]

    def up(zp, c):
        ref = piece(zp, x, c)
        return remote(ref, ref, send.at[0, zp, c], recv_z.at[zp, c], (2 * (z + 1) + x, s))

    def down(zp, c):
        ref = piece(zp, x, c)
        return remote(ref, ref, send.at[1, zp, c], recv_z.at[zp, c], (2 * (z - 1) + x, s))

    def across(zp, c):
        ref = piece(zp, x, c)
        return remote(ref, ref, send.at[2, zp, c], recv_x.at[zp, c], (2 * z + 1 - x, s))

    def to_share(k):
        ref = row.at[s]
        return remote(ref, ref, s_send.at[k], s_recv.at[s], (d, lax.rem(s + k, SEQ)))

    def from_share(k):
        other = lax.rem(s + k, SEQ)
        ref = row.at[other]
        return remote(ref, ref, s_send.at[k], s_recv.at[other], (d, other))

    def to_group(k):
        return remote(
            row, shared_all.at[d], d_send.at[k], d_recv.at[d], (lax.rem(d + k, DP), s)
        )

    def from_group(k):
        other = lax.rem(d + k, DP)
        return remote(row, shared_all.at[other], d_send.at[k], d_recv.at[other], (other, s))

    for k in range(1, SEQ):
        to_share(k).start()
    for c in range(parts):
        pl.when(z < Z - 1)(lambda: up(z, c).start())
        pl.when(z > 0)(lambda: down(z, c).start())
        across(z, c).start()
    for k in range(1, SEQ):
        from_share(k).wait_recv()
    shared_all[d] = row[...]
    for k in range(1, DP):
        to_group(k).start()
    for k in range(1, Z):
        for c in range(parts):

            @pl.when(z >= k)
            def _():
                up(z - k, c).wait_recv()
                pl.when(z < Z - 1)(lambda: up(z - k, c).start())
                across(z - k, c).start()

            @pl.when(z + k < Z)
            def _():
                down(z + k, c).wait_recv()
                pl.when(z > 0)(lambda: down(z + k, c).start())
                across(z + k, c).start()

    for zp in range(Z):
        for c in range(parts):
            ref = piece(zp, 1 - x, c)
            remote(
                ref, ref, send.at[2, zp, c], recv_x.at[zp, c], (2 * z + 1 - x, s)
            ).wait_recv()
            across(zp, c).wait_send()
            pl.when((z >= zp) & (z < Z - 1))(lambda: up(zp, c).wait_send())
            pl.when((z <= zp) & (z > 0))(lambda: down(zp, c).wait_send())
    for k in range(1, SEQ):
        to_share(k).wait_send()
    for k in range(1, DP):
        to_group(k).wait_send()
        from_group(k).wait_recv()
    for k in range(1, DP):
        head = full[k * BLOCK : k * BLOCK + EDGE, :].astype(jnp.float32)
        tail = tails[k - 1].astype(jnp.float32)
        full[k * BLOCK : k * BLOCK + EDGE, :] = (head + tail).astype(jnp.bfloat16)
    full[DP * BLOCK :, :] = tails[DP - 1]


def gather_parts(split_params, shared_params, dp_count, seq_count):
    rows = split_params.shape[1] // LANES
    mine = split_params.reshape(rows, 1, LANES)
    count = shared_params.shape[0]
    padded = jnp.pad(shared_params, (0, SHARED_ROWS * LANES - count))
    vmem = pl.BlockSpec(memory_space=pltpu.VMEM)
    parts = len(GATHER_CHUNKS) + 1
    dma = pltpu.SemaphoreType.DMA
    full, shared_all = pl.pallas_call(
        gather_kernel,
        out_shape=(
            jax.ShapeDtypeStruct((DP * BLOCK + EDGE, LANES), jnp.bfloat16),
            jax.ShapeDtypeStruct((DP, SEQ, SHARED_ROWS, LANES), jnp.float32),
        ),
        in_specs=[pl.BlockSpec(memory_space=pl.ANY), vmem],
        out_specs=(vmem, vmem),
        scratch_shapes=[
            dma,
            pltpu.VMEM((rows, LANES), jnp.float32),
            pltpu.VMEM((SPAN, LANES), jnp.float32),
            pltpu.VMEM((DP, EDGE, LANES), jnp.bfloat16),
            pltpu.VMEM((SEQ, SHARED_ROWS, LANES), jnp.float32),
            dma((3, Z, parts)),
            dma((Z, parts)),
            dma((Z, parts)),
            dma((SEQ,)),
            dma((SEQ,)),
            dma((DP,)),
            dma((DP,)),
        ],
        compiler_params=pltpu.CompilerParams(
            collective_id=0, has_side_effects=True, vmem_limit_bytes=24 * 2**20
        ),
        cost_estimate=pl.CostEstimate(flops=0, bytes_accessed=200 * 2**20, transcendentals=0),
        name="gather_params",
    )(mine, padded.reshape(SHARED_ROWS, LANES))
    shared_full = shared_all.reshape(DP * SEQ, SHARED_ROWS * LANES)[:, :count].reshape(-1)
    return full, shared_full


def reduce_kernel(
    flat,
    shared,
    out,
    shared_out,
    x_in,
    up_in,
    down_in,
    stage,
    share_in,
    share_sum,
    group_in,
    x_send,
    x_recv,
    z_send,
    up_recv,
    down_recv,
    s_send,
    s_recv,
    d_send,
    d_recv,
):
    d, s = lax.axis_index("dp"), lax.axis_index("seq")
    z, x = d // 2, lax.rem(d, 2)
    f32 = jnp.float32
    enter(d, s)

    def across(zp, c):
        offset, size = REDUCE_CHUNKS[c]
        start = pl.multiple_of((2 * zp + 1 - x) * BLOCK + offset, EDGE)
        return remote(
            flat.at[pl.ds(start, size)],
            x_in.at[zp, pl.ds(offset, size)],
            x_send.at[zp, c],
            x_recv.at[zp, c],
            (2 * z + 1 - x, s),
        )

    def along(zp, c, step, into, recv):
        offset, size = REDUCE_CHUNKS[c]
        return remote(
            stage.at[zp, pl.ds(offset, size)],
            into.at[zp, pl.ds(offset, size)],
            z_send.at[zp, c],
            recv.at[zp, c],
            (2 * (z + step) + x, s),
        )

    def up(zp, c):
        return along(zp, c, 1, up_in, up_recv)

    def down(zp, c):
        return along(zp, c, -1, down_in, down_recv)

    def add(zp, c, others, store):
        offset, size = REDUCE_CHUNKS[c]
        tile = 112 if size % 128 else 128

        def body(k, carry):
            at = pl.multiple_of(offset + k * tile, EDGE)
            own = pl.multiple_of((2 * zp + x) * BLOCK + offset + k * tile, EDGE)
            total = flat[pl.ds(own, tile), :].astype(f32)
            for ref in (x_in, *others):
                total = total + ref[zp, pl.ds(at, tile), :].astype(f32)
            store(at, tile, total)
            return carry

        lax.fori_loop(0, size // tile, body, 0)

    def hop(zp, c, others, copy):
        def store(at, tile, total):
            stage[zp, pl.ds(at, tile), :] = total.astype(jnp.bfloat16)

        add(zp, c, others, store)
        copy.start()

    def to_share(k):
        other = lax.rem(s + k, SEQ)
        return remote(
            shared.at[other], share_in.at[s], s_send.at[k], s_recv.at[s], (d, other)
        )

    def from_share(k):
        other = lax.rem(s + k, SEQ)
        return remote(
            shared.at[s], share_in.at[other], s_send.at[k], s_recv.at[other], (d, other)
        )

    def to_group(k):
        other = lax.rem(d + k, DP)
        return remote(
            share_sum.at[other], group_in.at[d], d_send.at[k], d_recv.at[d], (other, s)
        )

    def from_group(k):
        other = lax.rem(d + k, DP)
        return remote(
            share_sum.at[d], group_in.at[other], d_send.at[k], d_recv.at[other], (other, s)
        )

    chunks = range(len(REDUCE_CHUNKS))
    items = [(zp, c) for c in chunks for zp in (Z - 1, 0)]
    items += [(zp, c) for c in chunks for zp in (2, 1)]
    ahead = 6
    for k in range(1, SEQ):
        to_share(k).start()
    for zp, c in items[:ahead]:
        across(zp, c).start()
    share_in[s] = shared[s]
    for k in range(1, SEQ):
        from_share(k).wait_recv()
    share_sum[...] = share_in[0] + share_in[1] + share_in[2] + share_in[3]
    for k in range(1, DP):
        to_group(k).start()
    group_in[d] = share_sum[d]

    for t, (zp, c) in enumerate(items):
        if t + ahead < len(items):
            across(*items[t + ahead]).start()

        @pl.when(z != zp)
        def _():
            across(zp, c).wait_recv()

        if zp > 0:

            @pl.when(z == 0)
            def _():
                hop(zp, c, (), up(zp, c))

        if zp > 1:

            @pl.when((z > 0) & (z < zp))
            def _():
                up(zp, c).wait_recv()
                hop(zp, c, (up_in,), up(zp, c))

        if zp < Z - 1:

            @pl.when(z == Z - 1)
            def _():
                hop(zp, c, (), down(zp, c))

        if zp < Z - 2:

            @pl.when((z < Z - 1) & (z > zp))
            def _():
                down(zp, c).wait_recv()
                hop(zp, c, (down_in,), down(zp, c))

    def keep(at, tile, total):
        out[pl.ds(at, tile), :] = total

    out[SPAN:, :] = jnp.zeros((SUM_ROWS - SPAN, LANES), f32)
    for c in chunks:
        across(z, c).wait_recv()

        @pl.when(z == 0)
        def _():
            down(z, c).wait_recv()
            add(z, c, (down_in,), keep)

        @pl.when(z == Z - 1)
        def _():
            up(z, c).wait_recv()
            add(z, c, (up_in,), keep)

        @pl.when((z > 0) & (z < Z - 1))
        def _():
            up(z, c).wait_recv()
            down(z, c).wait_recv()
            add(z, c, (up_in, down_in), keep)

    for zp, c in items:
        across(zp, c).wait_send()
        pl.when(z < zp)(lambda: up(zp, c).wait_send())
        pl.when(z > zp)(lambda: down(zp, c).wait_send())
    for k in range(1, SEQ):
        to_share(k).wait_send()
    for k in range(1, DP):
        to_group(k).wait_send()
        from_group(k).wait_recv()
    total = group_in[0]
    for k in range(1, DP):
        total = total + group_in[k]
    shared_out[...] = total


def reduce_parts(flat, shared_flat, dp_count, seq_count):
    count = shared_flat.shape[0] // (DP * SEQ)
    flat = jnp.pad(flat, ((0, DP * BLOCK + EDGE - flat.shape[0]), (0, 0)))
    shared = jnp.pad(
        shared_flat.reshape(DP, SEQ, count), ((0, 0), (0, 0), (0, SHARED_ROWS * LANES - count))
    )
    shared = shared.transpose(1, 0, 2).reshape(SEQ, DP, SHARED_ROWS, LANES)
    vmem = pl.BlockSpec(memory_space=pltpu.VMEM)
    dma = pltpu.SemaphoreType.DMA
    held = pltpu.VMEM((Z, SPAN, LANES), jnp.bfloat16)
    sems = dma((Z, len(REDUCE_CHUNKS)))
    out, shared_out = pl.pallas_call(
        reduce_kernel,
        out_shape=(
            jax.ShapeDtypeStruct((SUM_ROWS, LANES), jnp.float32),
            jax.ShapeDtypeStruct((SHARED_ROWS, LANES), jnp.float32),
        ),
        in_specs=[vmem, vmem],
        out_specs=(vmem, vmem),
        scratch_shapes=[
            held,
            held,
            held,
            held,
            pltpu.VMEM((SEQ, DP, SHARED_ROWS, LANES), jnp.float32),
            pltpu.VMEM((DP, SHARED_ROWS, LANES), jnp.float32),
            pltpu.VMEM((DP, SHARED_ROWS, LANES), jnp.float32),
            sems,
            sems,
            sems,
            sems,
            sems,
            dma((SEQ,)),
            dma((SEQ,)),
            dma((DP,)),
            dma((DP,)),
        ],
        compiler_params=pltpu.CompilerParams(
            collective_id=1, has_side_effects=True, vmem_limit_bytes=40 * 2**20
        ),
        cost_estimate=pl.CostEstimate(flops=0, bytes_accessed=250 * 2**20, transcendentals=0),
        name="reduce_grads",
    )(flat, shared)
    return out, shared_out.reshape(-1)[:count]


def adamw_kernel(where, sums, *refs):
    sources, targets, held, results = refs[:3], refs[3:7], refs[7:10], refs[10:14]
    load, store = refs[14:]
    rows = held[0].shape[0]
    loads = [
        pltpu.make_async_copy(ref.at[:, 0, :], part, load.at[k])
        for k, (ref, part) in enumerate(zip(sources, held))
    ]
    for copy in loads:
        copy.start()
    for copy in loads:
        copy.wait()
    starts = list(range(0, rows, STEP_ROWS))
    stores = []
    for t, offset in enumerate(starts):
        size = min(STEP_ROWS, rows - offset)
        at = slice(offset, offset + size)
        grads = sums[pl.ds(where[0] + offset, size), :]
        values = (grads, *adamw(*(part[at, :] for part in held), grads))
        for k, value in enumerate(values):
            results[k][at, :] = value
            copy = pltpu.make_async_copy(
                results[k].at[at, :], targets[k].at[at, 0, :], store.at[k, t]
            )
            copy.start()
            stores.append(copy)
    for copy in stores:
        copy.wait()


def adamw_rows(sums, params, first_m, second_m):
    shape = params.shape
    rows = shape[1] // LANES
    hbm = pl.BlockSpec(memory_space=pl.ANY)
    dma = pltpu.SemaphoreType.DMA
    results = pl.pallas_call(
        adamw_kernel,
        out_shape=[jax.ShapeDtypeStruct((rows, 1, LANES), jnp.float32)] * 4,
        in_specs=[
            pl.BlockSpec(memory_space=pltpu.SMEM),
            pl.BlockSpec(memory_space=pltpu.VMEM),
            hbm,
            hbm,
            hbm,
        ],
        out_specs=[hbm] * 4,
        scratch_shapes=[pltpu.VMEM((rows, LANES), jnp.float32)] * 7
        + [dma((3,)), dma((4, pl.cdiv(rows, STEP_ROWS)))],
        compiler_params=pltpu.CompilerParams(vmem_limit_bytes=24 * 2**20),
        name="adamw_rows",
    )(
        lax.axis_index("dp").reshape(1),
        sums,
        *(part.reshape(rows, 1, LANES) for part in (params, first_m, second_m)),
    )
    return [part.reshape(shape) for part in results]


def attend(queries, keys_rot, values, segment_row):
    length = queries.shape[1]
    ids = jnp.arange(length, dtype=jnp.int32)
    allowed = (segment_row[:, None] == segment_row[None, :]) & (ids[:, None] >= ids[None, :])
    scores = jnp.einsum("hid,hjd->hij", queries, keys_rot, preferred_element_type=jnp.float32)
    scores = jnp.where(allowed[None], scores * HEAD_DIM ** (-0.5), masked_score)
    row_max = jnp.max(scores, -1, keepdims=True)
    log_total = row_max + jnp.log(jnp.sum(jnp.exp(scores - row_max), -1, keepdims=True))
    prob = jnp.exp(scores - log_total)
    prob_low = prob.astype(jnp.bfloat16)
    attended = jnp.einsum("hij,hjd->hid", prob_low, values, preferred_element_type=jnp.float32)
    return attended.astype(jnp.bfloat16), prob, prob_low


def attend_back(queries, keys_rot, values, attended, prob, prob_low, grad_att):
    delta = jnp.sum(grad_att.astype(jnp.float32) * attended.astype(jnp.float32), -1, keepdims=True)
    grad_values = jnp.einsum("hij,hid->hjd", prob_low, grad_att, preferred_element_type=jnp.float32)
    grad_prob = jnp.einsum("hid,hjd->hij", grad_att, values, preferred_element_type=jnp.float32)
    grad_scores = (prob * (grad_prob - delta) * HEAD_DIM ** (-0.5)).astype(jnp.bfloat16)
    grad_query = jnp.einsum(
        "hij,hjd->hid", grad_scores, keys_rot, preferred_element_type=jnp.float32
    )
    grad_keys = jnp.einsum("hij,hid->hjd", grad_scores, queries, preferred_element_type=jnp.float32)
    return grad_query, grad_keys, grad_values


def local_grouped(
    hidden_in,
    cotangent,
    segments,
    shared_params,
    split_params,
    shared_m1,
    split_m1,
    shared_m2,
    split_m2,
):
    dp_count = lax.axis_size("dp")
    seq_count = lax.axis_size("seq")
    share = lax.axis_index("seq")
    heads_here = HEADS // seq_count
    ql = 3 * MODEL_WIDTH // seq_count
    dl = MODEL_WIDTH // seq_count
    fl = FF // seq_count
    f32, bf16 = jnp.float32, jnp.bfloat16
    tokens_here = hidden_in.shape[0]
    both = lax.all_gather(
        jnp.concatenate([hidden_in, cotangent], 1), "seq", axis=0, tiled=True
    )
    group_hidden, group_cot = both[:, :MODEL_WIDTH], both[:, MODEL_WIDTH:]
    full, shared_full = gather_parts(split_params, shared_params, dp_count, seq_count)
    b_qkv, b_dense, b_proj, gain_one, shift_one, gain_two, shift_two = unpack_shared(shared_full)
    extents = share_layout(seq_count)
    offsets = [sum(extents[:k]) for k in range(6)]
    w_qkv, w_dense, w_fc, b_fc, w_proj = [
        full[offsets[k] : offsets[k + 1]].reshape(shape)
        for k, shape in enumerate(
            [(MODEL_WIDTH, ql), (dl, MODEL_WIDTH), (MODEL_WIDTH, fl), (fl,), (fl, MODEL_WIDTH)]
        )
    ]
    b_fc = b_fc.astype(f32)
    b_qkv_mine = lax.dynamic_slice(b_qkv, (share * ql,), (ql,))

    resid = group_hidden.astype(f32)
    first_norm, normed, root = layer_norm(resid, gain_one, shift_one)
    first_low = first_norm.astype(bf16)
    second_low = (normed * gain_two + shift_two).astype(bf16)
    length = resid.shape[0]

    qkv = (jnp.dot(first_low, w_qkv, preferred_element_type=f32) + b_qkv_mine).astype(bf16)
    qkv = qkv.reshape(length, heads_here, 3, HEAD_DIM).transpose(2, 1, 0, 3)
    segment_row = segments[0]
    cosines, sines = rotary_tables(segment_row)
    cosines, sines = cosines[:, 0], sines[:, 0]
    queries = rotate(qkv[0].astype(f32), cosines, sines, 1.0).astype(bf16)
    keys_rot = rotate(qkv[1].astype(f32), cosines, sines, 1.0).astype(bf16)
    values = qkv[2]
    attended, prob, prob_low = attend(queries, keys_rot, values, segment_row)
    att_flat = attended.transpose(1, 0, 2).reshape(length, dl)

    hidden_pre = jnp.dot(second_low, w_fc, preferred_element_type=f32) + b_fc
    activated = jax.nn.gelu(hidden_pre, approximate=False).astype(bf16)
    branch = jnp.dot(att_flat, w_dense, preferred_element_type=f32) + jnp.dot(
        activated, w_proj, preferred_element_type=f32
    )
    total = lax.psum_scatter(branch, "seq", scatter_dimension=0, tiled=True)
    output = (hidden_in.astype(f32) + total + b_dense + b_proj).astype(bf16)

    grad_outf = cotangent.astype(f32)
    grad_b_out = jnp.sum(grad_outf, 0)
    grad_w_proj = jnp.dot(activated.T, group_cot, preferred_element_type=f32)
    grad_hidden = jnp.dot(group_cot, w_proj.T, preferred_element_type=f32) * gelu_slope(hidden_pre)
    grad_b_fc = jnp.sum(grad_hidden, 0)
    grad_hidden_low = grad_hidden.astype(bf16)
    grad_w_fc = jnp.dot(second_low.T, grad_hidden_low, preferred_element_type=f32)
    grad_second = jnp.dot(grad_hidden_low, w_fc.T, preferred_element_type=f32)
    grad_w_dense = jnp.dot(att_flat.T, group_cot, preferred_element_type=f32)
    grad_att = (
        jnp.dot(group_cot, w_dense.T, preferred_element_type=f32)
        .astype(bf16)
        .reshape(length, heads_here, HEAD_DIM)
        .transpose(1, 0, 2)
    )
    grad_query, grad_keys, grad_values = attend_back(
        queries, keys_rot, values, attended, prob, prob_low, grad_att
    )
    grad_query = rotate(grad_query, cosines, sines, -1.0)
    grad_keys = rotate(grad_keys, cosines, sines, -1.0)
    grad_qkv = (
        jnp.stack([grad_query, grad_keys, grad_values])
        .astype(bf16)
        .transpose(2, 1, 0, 3)
        .reshape(length, ql)
    )
    grad_b_qkv = jnp.sum(grad_qkv.astype(f32), 0)
    grad_w_qkv = jnp.dot(first_low.T, grad_qkv, preferred_element_type=f32)
    grad_first = jnp.dot(grad_qkv, w_qkv.T, preferred_element_type=f32)

    scaled = lax.psum_scatter(
        gain_one * grad_first + gain_two * grad_second, "seq", scatter_dimension=0, tiled=True
    )
    normed_mine = lax.dynamic_slice(normed, (share * tokens_here, 0), (tokens_here, MODEL_WIDTH))
    root_mine = lax.dynamic_slice(root, (share * tokens_here, 0), (tokens_here, 1))
    input_grad = grad_outf + norm_back(scaled, 1.0, normed_mine, root_mine)

    shared_flat = jnp.concatenate(
        [
            lax.dynamic_update_slice(
                jnp.zeros((3 * MODEL_WIDTH,), f32), grad_b_qkv, (share * ql,)
            ),
            grad_b_out,
            grad_b_out,
            jnp.sum(grad_first * normed, 0),
            jnp.sum(grad_first, 0),
            jnp.sum(grad_second * normed, 0),
            jnp.sum(grad_second, 0),
        ]
    )
    flat = jnp.concatenate(
        [
            part.astype(bf16).reshape(-1, LANES)
            for part in (grad_w_qkv, grad_w_dense, grad_w_fc, grad_b_fc, grad_w_proj)
        ]
    )
    split_sums, shared_grads = reduce_parts(flat, shared_flat, dp_count, seq_count)
    shared_new, shared_m1_new, shared_m2_new = adamw(
        shared_params, shared_m1, shared_m2, shared_grads
    )
    split_grads, split_new, split_m1_new, split_m2_new = adamw_rows(
        split_sums, split_params, split_m1, split_m2
    )
    return (
        output,
        input_grad,
        shared_grads,
        split_grads,
        shared_new,
        split_new,
        shared_m1_new,
        split_m1_new,
        shared_m2_new,
        split_m2_new,
    )


def solution(mesh):
    in_specs = (
        P(("dp", "seq"), None),
        P(("dp", "seq"), None),
        P("dp", None),
        P(("dp", "seq")),
        P("seq", "dp"),
        P(("dp", "seq")),
        P("seq", "dp"),
        P(("dp", "seq")),
        P("seq", "dp"),
    )
    out_specs = (
        P(("dp", "seq"), None),
        P(("dp", "seq"), None),
        P(("dp", "seq")),
        P("seq", "dp"),
        P(("dp", "seq")),
        P("seq", "dp"),
        P(("dp", "seq")),
        P("seq", "dp"),
        P(("dp", "seq")),
        P("seq", "dp"),
    )
    dp_count, seq_count = mesh.shape["dp"], mesh.shape["seq"]
    local = local_grouped if (dp_count, seq_count) == (DP, SEQ) else local_general
    return jax.shard_map(local, mesh=mesh, in_specs=in_specs, out_specs=out_specs, check_vma=False)
```

```python
import math

import jax
import jax.numpy as jnp
from jax import lax
from jax.experimental import pallas as pl
from jax.experimental.pallas import tpu as pltpu
from jax.sharding import PartitionSpec as P

MODEL_WIDTH = 1024
HEADS = 16
HEAD_DIM = 64
FF = 4096
ROT = 16
STEP = 3


norm_eps = 1e-05
beta_first = 0.9
beta_second = 0.95
adam_eps = 1e-08
learn_rate = 0.1
weight_decay = 0.01
rotary_base = 10000.0
masked_score = -1e30


def unpack_shared(flat_vec):
    extents = [
        (3 * MODEL_WIDTH,),
        (MODEL_WIDTH,),
        (MODEL_WIDTH,),
        (MODEL_WIDTH,),
        (MODEL_WIDTH,),
        (MODEL_WIDTH,),
        (MODEL_WIDTH,),
    ]
    pieces = []
    offset = 0
    for extent in extents:
        number = math.prod(extent)
        pieces.append(flat_vec[offset : offset + number])
        offset = offset + number
    return pieces


def unpack_split(matrix, seq_count):
    rows = matrix.shape[0]
    qkv_part = 3 * MODEL_WIDTH // seq_count
    dense_output_slice = MODEL_WIDTH // seq_count
    hidden_units_slice = FF // seq_count
    zero_end = MODEL_WIDTH * qkv_part
    first_end = zero_end + dense_output_slice * MODEL_WIDTH
    second_end = first_end + MODEL_WIDTH * hidden_units_slice
    third_end = second_end + hidden_units_slice
    w_qkv = (
        matrix[:, :zero_end]
        .reshape(rows, MODEL_WIDTH, qkv_part)
        .transpose(1, 0, 2)
        .reshape(MODEL_WIDTH, rows * qkv_part)
    )
    dense_weight = matrix[:, zero_end:first_end].reshape(rows * dense_output_slice, MODEL_WIDTH)
    expand_weight = (
        matrix[:, first_end:second_end]
        .reshape(rows, MODEL_WIDTH, hidden_units_slice)
        .transpose(1, 0, 2)
        .reshape(MODEL_WIDTH, rows * hidden_units_slice)
    )
    b_fc = matrix[:, second_end:third_end].reshape(rows * hidden_units_slice)
    contract_weight = matrix[:, third_end:].reshape(rows * hidden_units_slice, MODEL_WIDTH)
    return (w_qkv, dense_weight, expand_weight, b_fc, contract_weight)


def pack_split(w_qkv, dense_weight, expand_weight, b_fc, contract_weight, seq_count):
    qkv_part = 3 * MODEL_WIDTH // seq_count
    dense_output_slice = MODEL_WIDTH // seq_count
    hidden_units_slice = FF // seq_count
    rows = dense_weight.shape[0] // dense_output_slice
    return jnp.concatenate(
        [
            w_qkv.reshape(MODEL_WIDTH, rows, qkv_part)
            .transpose(1, 0, 2)
            .reshape(rows, MODEL_WIDTH * qkv_part),
            dense_weight.reshape(rows, dense_output_slice * MODEL_WIDTH),
            expand_weight.reshape(MODEL_WIDTH, rows, hidden_units_slice)
            .transpose(1, 0, 2)
            .reshape(rows, MODEL_WIDTH * hidden_units_slice),
            b_fc.reshape(rows, hidden_units_slice),
            contract_weight.reshape(rows, hidden_units_slice * MODEL_WIDTH),
        ],
        1,
    )


def adamw(param_vals, first_m, second_m, grad_vals):
    first_new = beta_first * first_m + (1.0 - beta_first) * grad_vals
    second_new = beta_second * second_m + (1.0 - beta_second) * grad_vals * grad_vals
    first_hat = first_new / (1.0 - beta_first**STEP)
    second_hat = second_new / (1.0 - beta_second**STEP)
    param_new = param_vals - learn_rate * (
        first_hat / (jnp.sqrt(second_hat) + adam_eps) + weight_decay * param_vals
    )
    return (param_new, first_new, second_new)


def layer_norm(resid, gain_vec, shift_vec):
    average = jnp.mean(resid, -1, keepdims=True)
    centered = resid - average
    variance = jnp.mean(centered * centered, -1, keepdims=True)
    recip_root = lax.rsqrt(variance + norm_eps)
    normed = centered * recip_root
    return (normed * gain_vec + shift_vec, normed, recip_root)


def norm_back(grad_norm, gain_vec, normed, recip_root):
    scaled = grad_norm * gain_vec
    return recip_root * (
        scaled
        - jnp.mean(scaled, -1, keepdims=True)
        - normed * jnp.mean(scaled * normed, -1, keepdims=True)
    )


def gelu_slope(inputs):
    normal_cdf = 0.5 * (1.0 + jax.scipy.special.erf(inputs * 0.7071067811865476))
    return normal_cdf + inputs * jnp.exp(-0.5 * inputs * inputs) * 0.3989422804014327


def rotary_tables(segment_row):
    indices = jnp.arange(segment_row.shape[0], dtype=jnp.int32)
    change = jnp.concatenate([jnp.ones((1,), dtype=jnp.bool_), segment_row[1:] != segment_row[:-1]])
    starts = lax.cummax(jnp.where(change, indices, jnp.zeros_like(indices)), axis=0)
    positions = (indices - starts).astype(jnp.float32)
    frequency = rotary_base ** (-jnp.arange(0, ROT, 2, dtype=jnp.float32) / ROT)
    angles = positions[:, None] * frequency[None, :]
    return (jnp.cos(angles)[:, None, :], jnp.sin(angles)[:, None, :])


def rotate(field, cosines, sines, direction):
    half_rot = ROT // 2
    first_half = field[..., :half_rot]
    second = field[..., half_rot:ROT]
    return jnp.concatenate(
        [
            first_half * cosines - direction * second * sines,
            second * cosines + direction * first_half * sines,
            field[..., ROT:],
        ],
        -1,
    )


def score_block(query_block, keys_rot, seg_block, row_ids, segment_row, col_ids):
    scale = HEAD_DIM ** (-0.5)
    scores = (
        jnp.einsum("ihd,jhd->hij", query_block, keys_rot, preferred_element_type=jnp.float32)
        * scale
    )
    allowed = (seg_block[:, None] == segment_row[None, :]) & (row_ids[:, None] >= col_ids[None, :])
    return jnp.where(allowed[None], scores, masked_score)


def attention_forward(queries, keys_rot, values, segment_row):
    segment_length, heads_here, head_size = queries.shape
    block_rows = min(512, segment_length)
    block_count = segment_length // block_rows
    col_ids = jnp.arange(segment_length, dtype=jnp.int32)

    def one_block(packed):
        query_block, seg_block, row_ids = packed
        scores = score_block(query_block, keys_rot, seg_block, row_ids, segment_row, col_ids)
        row_max = jnp.max(scores, -1, keepdims=True)
        log_total = row_max[..., 0] + jnp.log(jnp.sum(jnp.exp(scores - row_max), -1))
        probability = jnp.exp(scores - log_total[..., None]).astype(jnp.bfloat16)
        attended = jnp.einsum(
            "hij,jhd->ihd", probability, values, preferred_element_type=jnp.float32
        ).astype(jnp.bfloat16)
        return (attended, log_total)

    attended, log_totals = lax.map(
        one_block,
        (
            queries.reshape(block_count, block_rows, heads_here, head_size),
            segment_row.reshape(block_count, block_rows),
            col_ids.reshape(block_count, block_rows),
        ),
    )
    return (attended.reshape(segment_length, heads_here, head_size), log_totals)


def attention_backward(queries, keys_rot, values, attended, log_totals, grad_att, segment_row):
    segment_length, heads_here, head_size = queries.shape
    block_rows = min(512, segment_length)
    block_count = segment_length // block_rows
    col_ids = jnp.arange(segment_length, dtype=jnp.int32)
    scale = HEAD_DIM ** (-0.5)

    def one_block(running, packed):
        grad_keys, grad_values = running
        query_block, out_block, grad_block, log_total, seg_block, row_ids = packed
        scores = score_block(query_block, keys_rot, seg_block, row_ids, segment_row, col_ids)
        probability = jnp.exp(scores - log_total[..., None])
        prob_low = probability.astype(jnp.bfloat16)
        delta = jnp.sum(grad_block.astype(jnp.float32) * out_block.astype(jnp.float32), -1).T
        grad_values = grad_values + jnp.einsum(
            "hij,ihd->jhd", prob_low, grad_block, preferred_element_type=jnp.float32
        )
        grad_prob = jnp.einsum(
            "ihd,jhd->hij", grad_block, values, preferred_element_type=jnp.float32
        )
        grad_scores = (probability * (grad_prob - delta[..., None]) * scale).astype(jnp.bfloat16)
        grad_query = jnp.einsum(
            "hij,jhd->ihd", grad_scores, keys_rot, preferred_element_type=jnp.float32
        )
        grad_keys = grad_keys + jnp.einsum(
            "hij,ihd->jhd", grad_scores, query_block, preferred_element_type=jnp.float32
        )
        return ((grad_keys, grad_values), grad_query)

    zero_field = jnp.zeros((segment_length, heads_here, head_size), jnp.float32)
    shaped = (
        queries.reshape(block_count, block_rows, heads_here, head_size),
        attended.reshape(block_count, block_rows, heads_here, head_size),
        grad_att.reshape(block_count, block_rows, heads_here, head_size),
        log_totals,
        segment_row.reshape(block_count, block_rows),
        col_ids.reshape(block_count, block_rows),
    )
    (grad_keys, grad_values), grad_query = lax.scan(one_block, (zero_field, zero_field), shaped)
    return (grad_query.reshape(segment_length, heads_here, head_size), grad_keys, grad_values)


def local_general(
    hidden_in,
    cotangent,
    segments,
    shared_params,
    split_params,
    shared_m1,
    split_m1,
    shared_m2,
    split_m2,
):
    tokens_here = hidden_in.shape[0]
    seq_count = lax.axis_size("seq")
    heads_here = HEADS // seq_count
    qkv_cols = 3 * MODEL_WIDTH // seq_count
    shared_full = lax.all_gather(shared_params, ("dp", "seq"), axis=0, tiled=True)
    b_qkv, b_dense, b_proj, gain_one, shift_one, gain_two, shift_two = unpack_shared(shared_full)
    split_mine = lax.all_gather(split_params.astype(jnp.bfloat16), "dp", axis=1, tiled=True)
    w_qkv_share, dense_weight, expand_weight, b_fc, contract_weight = unpack_split(
        split_mine, seq_count
    )
    b_fc = b_fc.astype(jnp.float32)
    column_rows = lax.all_gather(split_mine[:, : MODEL_WIDTH * qkv_cols], "seq", axis=0, tiled=True)
    w_qkv = (
        column_rows.reshape(seq_count, MODEL_WIDTH, qkv_cols)
        .transpose(1, 0, 2)
        .reshape(MODEL_WIDTH, 3 * MODEL_WIDTH)
    )
    resid = hidden_in.astype(jnp.float32)
    first_norm, normed_one, root_one = layer_norm(resid, gain_one, shift_one)
    second_norm, normed_two, root_two = layer_norm(resid, gain_two, shift_two)
    first_low = first_norm.astype(jnp.bfloat16)
    second_low = second_norm.astype(jnp.bfloat16)
    group_first, group_norm, group_cot = (
        lax.all_gather(first_low, "seq", axis=0, tiled=True),
        lax.all_gather(second_low, "seq", axis=0, tiled=True),
        lax.all_gather(cotangent, "seq", axis=0, tiled=True),
    )
    group_length = group_first.shape[0]
    qkv = (
        (jnp.dot(first_low, w_qkv, preferred_element_type=jnp.float32) + b_qkv)
        .astype(jnp.bfloat16)
        .reshape(tokens_here, HEADS, 3 * HEAD_DIM)
    )
    grouped = lax.all_to_all(qkv, "seq", split_axis=1, concat_axis=0, tiled=True)
    segment_row = segments[0]
    cosines, sines = rotary_tables(segment_row)
    queries = rotate(grouped[..., :HEAD_DIM].astype(jnp.float32), cosines, sines, 1.0).astype(
        jnp.bfloat16
    )
    keys_rot = rotate(
        grouped[..., HEAD_DIM : 2 * HEAD_DIM].astype(jnp.float32), cosines, sines, 1.0
    ).astype(jnp.bfloat16)
    values = grouped[..., 2 * HEAD_DIM :]
    attended, log_totals = attention_forward(queries, keys_rot, values, segment_row)
    grad_outf = cotangent.astype(jnp.float32)
    grad_b_proj = jnp.sum(grad_outf, 0)
    grad_b_dense = jnp.sum(grad_outf, 0)
    att_flat = attended.reshape(group_length, heads_here * HEAD_DIM)
    hidden_pre = jnp.dot(group_norm, expand_weight, preferred_element_type=jnp.float32) + b_fc
    hidden_activations = jax.nn.gelu(hidden_pre, approximate=False).astype(jnp.bfloat16)
    branch = jnp.dot(att_flat, dense_weight, preferred_element_type=jnp.float32) + jnp.dot(
        hidden_activations, contract_weight, preferred_element_type=jnp.float32
    )
    total = (
        resid + lax.psum_scatter(branch, "seq", scatter_dimension=0, tiled=True) + b_dense + b_proj
    )
    output = total.astype(jnp.bfloat16)
    grad_w_proj = jnp.dot(hidden_activations.T, group_cot, preferred_element_type=jnp.float32)
    grad_hidden = jnp.dot(
        group_cot, contract_weight.T, preferred_element_type=jnp.float32
    ) * gelu_slope(hidden_pre)
    grad_b_fc = jnp.sum(grad_hidden, 0)
    hidden_reduced_precision = grad_hidden.astype(jnp.bfloat16)
    grad_w_fc = jnp.dot(group_norm.T, hidden_reduced_precision, preferred_element_type=jnp.float32)
    grad_second = lax.psum_scatter(
        jnp.dot(hidden_reduced_precision, expand_weight.T, preferred_element_type=jnp.float32),
        "seq",
        scatter_dimension=0,
        tiled=True,
    )
    grad_w_dense = jnp.dot(att_flat.T, group_cot, preferred_element_type=jnp.float32)
    grad_att_heads = (
        jnp.dot(group_cot, dense_weight.T, preferred_element_type=jnp.float32)
        .astype(jnp.bfloat16)
        .reshape(group_length, heads_here, HEAD_DIM)
    )
    grad_query, grad_keys, grad_values = attention_backward(
        queries, keys_rot, values, attended, log_totals, grad_att_heads, segment_row
    )
    grad_query = rotate(grad_query, cosines, sines, -1.0)
    grad_keys = rotate(grad_keys, cosines, sines, -1.0)
    grad_grouped = jnp.concatenate([grad_query, grad_keys, grad_values], -1).astype(jnp.bfloat16)
    grad_w_qkv_share = jnp.dot(
        group_first.T,
        grad_grouped.reshape(group_length, qkv_cols),
        preferred_element_type=jnp.float32,
    )
    grad_qkv = lax.all_to_all(grad_grouped, "seq", split_axis=0, concat_axis=1, tiled=True).reshape(
        tokens_here, 3 * MODEL_WIDTH
    )
    grad_b_qkv = jnp.sum(grad_qkv.astype(jnp.float32), 0)
    grad_first = jnp.dot(grad_qkv, w_qkv.T, preferred_element_type=jnp.float32)
    grad_gain_one = jnp.sum(grad_first * normed_one, 0)
    grad_shift_one = jnp.sum(grad_first, 0)
    grad_gain_two = jnp.sum(grad_second * normed_two, 0)
    grad_shift_two = jnp.sum(grad_second, 0)
    input_grad = (
        grad_outf
        + norm_back(grad_first, gain_one, normed_one, root_one)
        + norm_back(grad_second, gain_two, normed_two, root_two)
    )
    shared_flat = jnp.concatenate(
        [
            grad_b_qkv,
            grad_b_dense,
            grad_b_proj,
            grad_gain_one,
            grad_shift_one,
            grad_gain_two,
            grad_shift_two,
        ]
    )
    shared_grads = lax.psum_scatter(shared_flat, ("dp", "seq"), scatter_dimension=0, tiled=True)
    split_local = pack_split(
        grad_w_qkv_share, grad_w_dense, grad_w_fc, grad_b_fc, grad_w_proj, seq_count
    )
    split_grads = lax.psum_scatter(split_local, "dp", scatter_dimension=1, tiled=True)
    shared_new, shared_m1_new, shared_m2_new = adamw(
        shared_params, shared_m1, shared_m2, shared_grads
    )
    split_new, split_m1_new, split_m2_new = adamw(split_params, split_m1, split_m2, split_grads)
    return (
        output,
        input_grad,
        shared_grads,
        split_grads,
        shared_new,
        split_new,
        shared_m1_new,
        split_m1_new,
        shared_m2_new,
        split_m2_new,
    )


LANES = 128


def share_layout(seq_count):
    ql = 3 * MODEL_WIDTH // seq_count
    dl = MODEL_WIDTH // seq_count
    fl = FF // seq_count
    return [
        MODEL_WIDTH * ql // LANES,
        dl * MODEL_WIDTH // LANES,
        MODEL_WIDTH * fl // LANES,
        fl // LANES,
        fl * MODEL_WIDTH // LANES,
    ]


Z = 4
DP = 2 * Z
SEQ = 4
BLOCK = 3072
EDGE = 16
SPAN = BLOCK + EDGE
MESH = pl.DeviceIdType.MESH
GATHER_CHUNKS = [(k * 768, 768) for k in range(4)]
REDUCE_CHUNKS = [(0, 784), (784, 768), (1552, 768), (2320, 768)]
SHARED_ROWS = 8
PLACE_ROWS = 256
STEP_ROWS = 448
CAST_ROWS = 464
SUM_ROWS = 7 * STEP_ROWS + EDGE


def enter(d, s):
    barrier = pltpu.get_barrier_semaphore()
    for k in range(1, DP):
        pl.semaphore_signal(
            barrier, inc=1, device_id=(lax.rem(d + k, DP), s), device_id_type=MESH
        )
    for k in range(1, SEQ):
        pl.semaphore_signal(
            barrier, inc=1, device_id=(d, lax.rem(s + k, SEQ)), device_id_type=MESH
        )
    pl.semaphore_wait(barrier, DP - 1 + SEQ - 1)


def remote(src, dst, send_sem, recv_sem, device):
    return pltpu.make_async_remote_copy(
        src_ref=src,
        dst_ref=dst,
        send_sem=send_sem,
        recv_sem=recv_sem,
        device_id=device,
        device_id_type=MESH,
    )


def gather_kernel(
    source, shared, full, shared_all, load, mine, placed, tails, row, send, recv_z, recv_x, s_send, s_recv, d_send, d_recv
):
    d, s = lax.axis_index("dp"), lax.axis_index("seq")
    z, x = d // 2, lax.rem(d, 2)
    parts = len(GATHER_CHUNKS) + 1
    fetch = pltpu.make_async_copy(source.at[:, 0, :], mine, load)
    fetch.start()
    fetch.wait()
    rows = mine.shape[0]
    edge = jnp.zeros((EDGE, LANES), jnp.float32)
    placed[:EDGE, :] = edge
    placed[BLOCK:, :] = edge
    for offset in range(0, rows, PLACE_ROWS):
        size = min(PLACE_ROWS, rows - offset)
        placed[pl.ds(d + offset, size), :] = mine[offset : offset + size, :]
    for offset in range(0, BLOCK, PLACE_ROWS):
        at = pl.multiple_of(d * BLOCK + offset, PLACE_ROWS)
        full[pl.ds(at, PLACE_ROWS), :] = placed[offset : offset + PLACE_ROWS, :].astype(full.dtype)
    tails[d] = placed[BLOCK:, :].astype(full.dtype)
    row[s] = shared[...]
    enter(d, s)

    def piece(zp, xp, c):
        if c == parts - 1:
            return tails.at[2 * zp + xp]
        offset, size = GATHER_CHUNKS[c]
        return full.at[pl.ds(pl.multiple_of((2 * zp + xp) * BLOCK + offset, 256), size)]

    def up(zp, c):
        ref = piece(zp, x, c)
        return remote(ref, ref, send.at[0, zp, c], recv_z.at[zp, c], (2 * (z + 1) + x, s))

    def down(zp, c):
        ref = piece(zp, x, c)
        return remote(ref, ref, send.at[1, zp, c], recv_z.at[zp, c], (2 * (z - 1) + x, s))

    def across(zp, c):
        ref = piece(zp, x, c)
        return remote(ref, ref, send.at[2, zp, c], recv_x.at[zp, c], (2 * z + 1 - x, s))

    def to_share(k):
        ref = row.at[s]
        return remote(ref, ref, s_send.at[k], s_recv.at[s], (d, lax.rem(s + k, SEQ)))

    def from_share(k):
        other = lax.rem(s + k, SEQ)
        ref = row.at[other]
        return remote(ref, ref, s_send.at[k], s_recv.at[other], (d, other))

    def to_group(k):
        return remote(
            row, shared_all.at[d], d_send.at[k], d_recv.at[d], (lax.rem(d + k, DP), s)
        )

    def from_group(k):
        other = lax.rem(d + k, DP)
        return remote(row, shared_all.at[other], d_send.at[k], d_recv.at[other], (other, s))

    for k in range(1, SEQ):
        to_share(k).start()
    for c in range(parts):
        pl.when(z < Z - 1)(lambda: up(z, c).start())
        pl.when(z > 0)(lambda: down(z, c).start())
        across(z, c).start()
    for k in range(1, SEQ):
        from_share(k).wait_recv()
    shared_all[d] = row[...]
    for k in range(1, DP):
        to_group(k).start()
    for k in range(1, Z):
        for c in range(parts):

            @pl.when(z >= k)
            def _():
                up(z - k, c).wait_recv()
                pl.when(z < Z - 1)(lambda: up(z - k, c).start())
                across(z - k, c).start()

            @pl.when(z + k < Z)
            def _():
                down(z + k, c).wait_recv()
                pl.when(z > 0)(lambda: down(z + k, c).start())
                across(z + k, c).start()

    for zp in range(Z):
        for c in range(parts):
            ref = piece(zp, 1 - x, c)
            remote(
                ref, ref, send.at[2, zp, c], recv_x.at[zp, c], (2 * z + 1 - x, s)
            ).wait_recv()
            across(zp, c).wait_send()
            pl.when((z >= zp) & (z < Z - 1))(lambda: up(zp, c).wait_send())
            pl.when((z <= zp) & (z > 0))(lambda: down(zp, c).wait_send())
    for k in range(1, SEQ):
        to_share(k).wait_send()
    for k in range(1, DP):
        to_group(k).wait_send()
        from_group(k).wait_recv()
    for k in range(1, DP):
        head = full[k * BLOCK : k * BLOCK + EDGE, :].astype(jnp.float32)
        tail = tails[k - 1].astype(jnp.float32)
        full[k * BLOCK : k * BLOCK + EDGE, :] = (head + tail).astype(jnp.bfloat16)
    full[DP * BLOCK :, :] = tails[DP - 1]


def gather_parts(split_params, shared_params, dp_count, seq_count):
    rows = split_params.shape[1] // LANES
    mine = split_params.reshape(rows, 1, LANES)
    count = shared_params.shape[0]
    padded = jnp.pad(shared_params, (0, SHARED_ROWS * LANES - count))
    vmem = pl.BlockSpec(memory_space=pltpu.VMEM)
    parts = len(GATHER_CHUNKS) + 1
    dma = pltpu.SemaphoreType.DMA
    full, shared_all = pl.pallas_call(
        gather_kernel,
        out_shape=(
            jax.ShapeDtypeStruct((DP * BLOCK + EDGE, LANES), jnp.bfloat16),
            jax.ShapeDtypeStruct((DP, SEQ, SHARED_ROWS, LANES), jnp.float32),
        ),
        in_specs=[pl.BlockSpec(memory_space=pl.ANY), vmem],
        out_specs=(vmem, vmem),
        scratch_shapes=[
            dma,
            pltpu.VMEM((rows, LANES), jnp.float32),
            pltpu.VMEM((SPAN, LANES), jnp.float32),
            pltpu.VMEM((DP, EDGE, LANES), jnp.bfloat16),
            pltpu.VMEM((SEQ, SHARED_ROWS, LANES), jnp.float32),
            dma((3, Z, parts)),
            dma((Z, parts)),
            dma((Z, parts)),
            dma((SEQ,)),
            dma((SEQ,)),
            dma((DP,)),
            dma((DP,)),
        ],
        compiler_params=pltpu.CompilerParams(
            collective_id=0, has_side_effects=True, vmem_limit_bytes=24 * 2**20
        ),
        cost_estimate=pl.CostEstimate(flops=0, bytes_accessed=200 * 2**20, transcendentals=0),
        name="gather_params",
    )(mine, padded.reshape(SHARED_ROWS, LANES))
    shared_full = shared_all.reshape(DP * SEQ, SHARED_ROWS * LANES)[:, :count].reshape(-1)
    return full, shared_full


def reduce_kernel(
    grad_qkv,
    grad_dense,
    grad_fc,
    grad_bias,
    grad_proj,
    shared,
    out,
    shared_out,
    wide,
    flat,
    x_in,
    up_in,
    down_in,
    stage,
    share_in,
    share_sum,
    group_in,
    x_send,
    x_recv,
    z_send,
    up_recv,
    down_recv,
    s_send,
    s_recv,
    d_send,
    d_recv,
):
    d, s = lax.axis_index("dp"), lax.axis_index("seq")
    z, x = d // 2, lax.rem(d, 2)
    f32 = jnp.float32
    base = 0
    for ref in (grad_qkv, grad_dense, grad_fc, grad_bias, grad_proj):
        count, across_row = ref.shape[0], ref.shape[1] // LANES
        tile = min(count, 256)

        def spread(k, carry, ref=ref, base=base, across_row=across_row, tile=tile):
            at = pl.multiple_of(k * tile, tile)
            to = base + k * tile * across_row
            for j in range(across_row):
                part = ref[pl.ds(at, tile), j * LANES : (j + 1) * LANES].astype(f32)
                if across_row == 1:
                    wide[pl.ds(to, tile), :] = part
                else:
                    wide[pl.ds(to + j, tile, stride=across_row), :] = part
            return carry

        lax.fori_loop(0, count // tile, spread, 0)
        base += count * across_row
    wide[base:, :] = jnp.zeros((wide.shape[0] - base, LANES), f32)

    def narrow(k, carry):
        at = pl.multiple_of(k * CAST_ROWS, EDGE)
        flat[pl.ds(at, CAST_ROWS), :] = wide[pl.ds(at, CAST_ROWS), :].astype(flat.dtype)
        return carry

    lax.fori_loop(0, wide.shape[0] // CAST_ROWS, narrow, 0)
    enter(d, s)

    def across(zp, c):
        offset, size = REDUCE_CHUNKS[c]
        start = pl.multiple_of((2 * zp + 1 - x) * BLOCK + offset, EDGE)
        return remote(
            flat.at[pl.ds(start, size)],
            x_in.at[zp, pl.ds(offset, size)],
            x_send.at[zp, c],
            x_recv.at[zp, c],
            (2 * z + 1 - x, s),
        )

    def along(zp, c, step, into, recv):
        offset, size = REDUCE_CHUNKS[c]
        return remote(
            stage.at[zp, pl.ds(offset, size)],
            into.at[zp, pl.ds(offset, size)],
            z_send.at[zp, c],
            recv.at[zp, c],
            (2 * (z + step) + x, s),
        )

    def up(zp, c):
        return along(zp, c, 1, up_in, up_recv)

    def down(zp, c):
        return along(zp, c, -1, down_in, down_recv)

    def add(zp, c, others, store):
        offset, size = REDUCE_CHUNKS[c]
        tile = 112 if size % 128 else 128

        def body(k, carry):
            at = pl.multiple_of(offset + k * tile, EDGE)
            own = pl.multiple_of((2 * zp + x) * BLOCK + offset + k * tile, EDGE)
            total = flat[pl.ds(own, tile), :].astype(f32)
            for ref in (x_in, *others):
                total = total + ref[zp, pl.ds(at, tile), :].astype(f32)
            store(at, tile, total)
            return carry

        lax.fori_loop(0, size // tile, body, 0)

    def hop(zp, c, others, copy):
        def store(at, tile, total):
            stage[zp, pl.ds(at, tile), :] = total.astype(jnp.bfloat16)

        add(zp, c, others, store)
        copy.start()

    def to_share(k):
        other = lax.rem(s + k, SEQ)
        return remote(
            shared.at[other], share_in.at[s], s_send.at[k], s_recv.at[s], (d, other)
        )

    def from_share(k):
        other = lax.rem(s + k, SEQ)
        return remote(
            shared.at[s], share_in.at[other], s_send.at[k], s_recv.at[other], (d, other)
        )

    def to_group(k):
        other = lax.rem(d + k, DP)
        return remote(
            share_sum.at[other], group_in.at[d], d_send.at[k], d_recv.at[d], (other, s)
        )

    def from_group(k):
        other = lax.rem(d + k, DP)
        return remote(
            share_sum.at[d], group_in.at[other], d_send.at[k], d_recv.at[other], (other, s)
        )

    chunks = range(len(REDUCE_CHUNKS))
    items = [(zp, c) for c in chunks for zp in (Z - 1, 0)]
    items += [(zp, c) for c in chunks for zp in (2, 1)]
    ahead = 6
    for k in range(1, SEQ):
        to_share(k).start()
    for zp, c in items[:ahead]:
        across(zp, c).start()
    share_in[s] = shared[s]
    for k in range(1, SEQ):
        from_share(k).wait_recv()
    share_sum[...] = share_in[0] + share_in[1] + share_in[2] + share_in[3]
    for k in range(1, DP):
        to_group(k).start()
    group_in[d] = share_sum[d]

    for t, (zp, c) in enumerate(items):
        if t + ahead < len(items):
            across(*items[t + ahead]).start()

        @pl.when(z != zp)
        def _():
            across(zp, c).wait_recv()

        if zp > 0:

            @pl.when(z == 0)
            def _():
                hop(zp, c, (), up(zp, c))

        if zp > 1:

            @pl.when((z > 0) & (z < zp))
            def _():
                up(zp, c).wait_recv()
                hop(zp, c, (up_in,), up(zp, c))

        if zp < Z - 1:

            @pl.when(z == Z - 1)
            def _():
                hop(zp, c, (), down(zp, c))

        if zp < Z - 2:

            @pl.when((z < Z - 1) & (z > zp))
            def _():
                down(zp, c).wait_recv()
                hop(zp, c, (down_in,), down(zp, c))

    def keep(at, tile, total):
        out[pl.ds(at, tile), :] = total

    out[SPAN:, :] = jnp.zeros((SUM_ROWS - SPAN, LANES), f32)
    for c in chunks:
        across(z, c).wait_recv()

        @pl.when(z == 0)
        def _():
            down(z, c).wait_recv()
            add(z, c, (down_in,), keep)

        @pl.when(z == Z - 1)
        def _():
            up(z, c).wait_recv()
            add(z, c, (up_in,), keep)

        @pl.when((z > 0) & (z < Z - 1))
        def _():
            up(z, c).wait_recv()
            down(z, c).wait_recv()
            add(z, c, (up_in, down_in), keep)

    for zp, c in items:
        across(zp, c).wait_send()
        pl.when(z < zp)(lambda: up(zp, c).wait_send())
        pl.when(z > zp)(lambda: down(zp, c).wait_send())
    for k in range(1, SEQ):
        to_share(k).wait_send()
    for k in range(1, DP):
        to_group(k).wait_send()
        from_group(k).wait_recv()
    total = group_in[0]
    for k in range(1, DP):
        total = total + group_in[k]
    shared_out[...] = total


def reduce_parts(parts, shared_flat, dp_count, seq_count):
    count = shared_flat.shape[0] // (DP * SEQ)
    shared = jnp.pad(
        shared_flat.reshape(DP, SEQ, count), ((0, 0), (0, 0), (0, SHARED_ROWS * LANES - count))
    )
    shared = shared.transpose(1, 0, 2).reshape(SEQ, DP, SHARED_ROWS, LANES)
    vmem = pl.BlockSpec(memory_space=pltpu.VMEM)
    dma = pltpu.SemaphoreType.DMA
    held = pltpu.VMEM((Z, SPAN, LANES), jnp.bfloat16)
    sems = dma((Z, len(REDUCE_CHUNKS)))
    out, shared_out = pl.pallas_call(
        reduce_kernel,
        out_shape=(
            jax.ShapeDtypeStruct((SUM_ROWS, LANES), jnp.float32),
            jax.ShapeDtypeStruct((SHARED_ROWS, LANES), jnp.float32),
        ),
        in_specs=[vmem] * 6,
        out_specs=(vmem, vmem),
        scratch_shapes=[
            pltpu.VMEM((DP * BLOCK + EDGE, LANES), jnp.float32),
            pltpu.VMEM((DP * BLOCK + EDGE, LANES), jnp.bfloat16),
            held,
            held,
            held,
            held,
            pltpu.VMEM((SEQ, DP, SHARED_ROWS, LANES), jnp.float32),
            pltpu.VMEM((DP, SHARED_ROWS, LANES), jnp.float32),
            pltpu.VMEM((DP, SHARED_ROWS, LANES), jnp.float32),
            sems,
            sems,
            sems,
            sems,
            sems,
            dma((SEQ,)),
            dma((SEQ,)),
            dma((DP,)),
            dma((DP,)),
        ],
        compiler_params=pltpu.CompilerParams(
            collective_id=1, has_side_effects=True, vmem_limit_bytes=52 * 2**20
        ),
        cost_estimate=pl.CostEstimate(flops=0, bytes_accessed=250 * 2**20, transcendentals=0),
        name="reduce_grads",
    )(*parts, shared)
    return out, shared_out.reshape(-1)[:count]


def adamw_kernel(where, sums, *refs):
    sources, targets, held, results = refs[:3], refs[3:7], refs[7:10], refs[10:14]
    load, store = refs[14:]
    rows = held[0].shape[0]
    loads = [
        pltpu.make_async_copy(ref.at[:, 0, :], part, load.at[k])
        for k, (ref, part) in enumerate(zip(sources, held))
    ]
    for copy in loads:
        copy.start()
    for copy in loads:
        copy.wait()
    starts = list(range(0, rows, STEP_ROWS))
    stores = []
    for t, offset in enumerate(starts):
        size = min(STEP_ROWS, rows - offset)
        at = slice(offset, offset + size)
        grads = sums[pl.ds(where[0] + offset, size), :]
        values = (grads, *adamw(*(part[at, :] for part in held), grads))
        for k, value in enumerate(values):
            results[k][at, :] = value
            copy = pltpu.make_async_copy(
                results[k].at[at, :], targets[k].at[at, 0, :], store.at[k, t]
            )
            copy.start()
            stores.append(copy)
    for copy in stores:
        copy.wait()


def adamw_rows(sums, params, first_m, second_m):
    shape = params.shape
    rows = shape[1] // LANES
    hbm = pl.BlockSpec(memory_space=pl.ANY)
    dma = pltpu.SemaphoreType.DMA
    results = pl.pallas_call(
        adamw_kernel,
        out_shape=[jax.ShapeDtypeStruct((rows, 1, LANES), jnp.float32)] * 4,
        in_specs=[
            pl.BlockSpec(memory_space=pltpu.SMEM),
            pl.BlockSpec(memory_space=pltpu.VMEM),
            hbm,
            hbm,
            hbm,
        ],
        out_specs=[hbm] * 4,
        scratch_shapes=[pltpu.VMEM((rows, LANES), jnp.float32)] * 7
        + [dma((3,)), dma((4, pl.cdiv(rows, STEP_ROWS)))],
        compiler_params=pltpu.CompilerParams(vmem_limit_bytes=24 * 2**20),
        name="adamw_rows",
    )(
        lax.axis_index("dp").reshape(1),
        sums,
        *(part.reshape(rows, 1, LANES) for part in (params, first_m, second_m)),
    )
    return [part.reshape(shape) for part in results]


def attend(queries, keys_rot, values, segment_row):
    length = queries.shape[1]
    ids = jnp.arange(length, dtype=jnp.int32)
    allowed = (segment_row[:, None] == segment_row[None, :]) & (ids[:, None] >= ids[None, :])
    scores = jnp.einsum("hid,hjd->hij", queries, keys_rot, preferred_element_type=jnp.float32)
    scores = jnp.where(allowed[None], scores * HEAD_DIM ** (-0.5), masked_score)
    row_max = jnp.max(scores, -1, keepdims=True)
    log_total = row_max + jnp.log(jnp.sum(jnp.exp(scores - row_max), -1, keepdims=True))
    prob = jnp.exp(scores - log_total)
    prob_low = prob.astype(jnp.bfloat16)
    attended = jnp.einsum("hij,hjd->hid", prob_low, values, preferred_element_type=jnp.float32)
    return attended.astype(jnp.bfloat16), prob, prob_low


def attend_back(queries, keys_rot, values, attended, prob, prob_low, grad_att):
    delta = jnp.sum(grad_att.astype(jnp.float32) * attended.astype(jnp.float32), -1, keepdims=True)
    grad_values = jnp.einsum("hij,hid->hjd", prob_low, grad_att, preferred_element_type=jnp.float32)
    grad_prob = jnp.einsum("hid,hjd->hij", grad_att, values, preferred_element_type=jnp.float32)
    grad_scores = (prob * (grad_prob - delta) * HEAD_DIM ** (-0.5)).astype(jnp.bfloat16)
    grad_query = jnp.einsum(
        "hij,hjd->hid", grad_scores, keys_rot, preferred_element_type=jnp.float32
    )
    grad_keys = jnp.einsum("hij,hid->hjd", grad_scores, queries, preferred_element_type=jnp.float32)
    return grad_query, grad_keys, grad_values


def local_grouped(
    hidden_in,
    cotangent,
    segments,
    shared_params,
    split_params,
    shared_m1,
    split_m1,
    shared_m2,
    split_m2,
):
    dp_count = lax.axis_size("dp")
    seq_count = lax.axis_size("seq")
    share = lax.axis_index("seq")
    heads_here = HEADS // seq_count
    ql = 3 * MODEL_WIDTH // seq_count
    dl = MODEL_WIDTH // seq_count
    fl = FF // seq_count
    f32, bf16 = jnp.float32, jnp.bfloat16
    tokens_here = hidden_in.shape[0]
    both = lax.all_gather(
        jnp.concatenate([hidden_in, cotangent], 1), "seq", axis=0, tiled=True
    )
    group_hidden, group_cot = both[:, :MODEL_WIDTH], both[:, MODEL_WIDTH:]
    full, shared_full = gather_parts(split_params, shared_params, dp_count, seq_count)
    b_qkv, b_dense, b_proj, gain_one, shift_one, gain_two, shift_two = unpack_shared(shared_full)
    extents = share_layout(seq_count)
    offsets = [sum(extents[:k]) for k in range(6)]
    w_qkv, w_dense, w_fc, b_fc, w_proj = [
        full[offsets[k] : offsets[k + 1]].reshape(shape)
        for k, shape in enumerate(
            [(MODEL_WIDTH, ql), (dl, MODEL_WIDTH), (MODEL_WIDTH, fl), (fl,), (fl, MODEL_WIDTH)]
        )
    ]
    b_fc = b_fc.astype(f32)
    b_qkv_mine = lax.dynamic_slice(b_qkv, (share * ql,), (ql,))

    resid = group_hidden.astype(f32)
    first_norm, normed, root = layer_norm(resid, gain_one, shift_one)
    first_low = first_norm.astype(bf16)
    second_low = (normed * gain_two + shift_two).astype(bf16)
    length = resid.shape[0]

    qkv = (jnp.dot(first_low, w_qkv, preferred_element_type=f32) + b_qkv_mine).astype(bf16)
    qkv = qkv.reshape(length, heads_here, 3, HEAD_DIM).transpose(2, 1, 0, 3)
    segment_row = segments[0]
    cosines, sines = rotary_tables(segment_row)
    cosines, sines = cosines[:, 0], sines[:, 0]
    queries = rotate(qkv[0].astype(f32), cosines, sines, 1.0).astype(bf16)
    keys_rot = rotate(qkv[1].astype(f32), cosines, sines, 1.0).astype(bf16)
    values = qkv[2]
    attended, prob, prob_low = attend(queries, keys_rot, values, segment_row)
    att_flat = attended.transpose(1, 0, 2).reshape(length, dl)

    hidden_pre = jnp.dot(second_low, w_fc, preferred_element_type=f32) + b_fc
    activated = jax.nn.gelu(hidden_pre, approximate=False).astype(bf16)
    branch = jnp.dot(att_flat, w_dense, preferred_element_type=f32) + jnp.dot(
        activated, w_proj, preferred_element_type=f32
    )
    total = lax.psum_scatter(branch, "seq", scatter_dimension=0, tiled=True)
    output = (hidden_in.astype(f32) + total + b_dense + b_proj).astype(bf16)

    grad_outf = cotangent.astype(f32)
    grad_b_out = jnp.sum(grad_outf, 0)
    grad_w_proj = jnp.dot(activated.T, group_cot, preferred_element_type=f32)
    grad_hidden = jnp.dot(group_cot, w_proj.T, preferred_element_type=f32) * gelu_slope(hidden_pre)
    grad_b_fc = jnp.sum(grad_hidden, 0)
    grad_hidden_low = grad_hidden.astype(bf16)
    grad_w_fc = jnp.dot(second_low.T, grad_hidden_low, preferred_element_type=f32)
    grad_second = jnp.dot(grad_hidden_low, w_fc.T, preferred_element_type=f32)
    grad_w_dense = jnp.dot(att_flat.T, group_cot, preferred_element_type=f32)
    grad_att = (
        jnp.dot(group_cot, w_dense.T, preferred_element_type=f32)
        .astype(bf16)
        .reshape(length, heads_here, HEAD_DIM)
        .transpose(1, 0, 2)
    )
    grad_query, grad_keys, grad_values = attend_back(
        queries, keys_rot, values, attended, prob, prob_low, grad_att
    )
    grad_query = rotate(grad_query, cosines, sines, -1.0)
    grad_keys = rotate(grad_keys, cosines, sines, -1.0)
    grad_qkv = (
        jnp.stack([grad_query, grad_keys, grad_values])
        .astype(bf16)
        .transpose(2, 1, 0, 3)
        .reshape(length, ql)
    )
    grad_b_qkv = jnp.sum(grad_qkv.astype(f32), 0)
    grad_w_qkv = jnp.dot(first_low.T, grad_qkv, preferred_element_type=f32)
    grad_first = jnp.dot(grad_qkv, w_qkv.T, preferred_element_type=f32)

    scaled = lax.psum_scatter(
        gain_one * grad_first + gain_two * grad_second, "seq", scatter_dimension=0, tiled=True
    )
    normed_mine = lax.dynamic_slice(normed, (share * tokens_here, 0), (tokens_here, MODEL_WIDTH))
    root_mine = lax.dynamic_slice(root, (share * tokens_here, 0), (tokens_here, 1))
    input_grad = grad_outf + norm_back(scaled, 1.0, normed_mine, root_mine)

    shared_flat = jnp.concatenate(
        [
            lax.dynamic_update_slice(
                jnp.zeros((3 * MODEL_WIDTH,), f32), grad_b_qkv, (share * ql,)
            ),
            grad_b_out,
            grad_b_out,
            jnp.sum(grad_first * normed, 0),
            jnp.sum(grad_first, 0),
            jnp.sum(grad_second * normed, 0),
            jnp.sum(grad_second, 0),
        ]
    )
    parts = [
        grad_w_qkv.astype(bf16),
        grad_w_dense.astype(bf16),
        grad_w_fc.astype(bf16),
        grad_b_fc.reshape(-1, LANES),
        grad_w_proj.astype(bf16),
    ]
    split_sums, shared_grads = reduce_parts(parts, shared_flat, dp_count, seq_count)
    shared_new, shared_m1_new, shared_m2_new = adamw(
        shared_params, shared_m1, shared_m2, shared_grads
    )
    split_grads, split_new, split_m1_new, split_m2_new = adamw_rows(
        split_sums, split_params, split_m1, split_m2
    )
    return (
        output,
        input_grad,
        shared_grads,
        split_grads,
        shared_new,
        split_new,
        shared_m1_new,
        split_m1_new,
        shared_m2_new,
        split_m2_new,
    )


def solution(mesh):
    in_specs = (
        P(("dp", "seq"), None),
        P(("dp", "seq"), None),
        P("dp", None),
        P(("dp", "seq")),
        P("seq", "dp"),
        P(("dp", "seq")),
        P("seq", "dp"),
        P(("dp", "seq")),
        P("seq", "dp"),
    )
    out_specs = (
        P(("dp", "seq"), None),
        P(("dp", "seq"), None),
        P(("dp", "seq")),
        P("seq", "dp"),
        P(("dp", "seq")),
        P("seq", "dp"),
        P(("dp", "seq")),
        P("seq", "dp"),
        P(("dp", "seq")),
        P("seq", "dp"),
    )
    dp_count, seq_count = mesh.shape["dp"], mesh.shape["seq"]
    local = local_grouped if (dp_count, seq_count) == (DP, SEQ) else local_general
    return jax.shard_map(local, mesh=mesh, in_specs=in_specs, out_specs=out_specs, check_vma=False)
```
